32 devices in a mesh: rep: 8 (over z, x), tp: 4 (over y, core).
Axes of the slice: x: 2, y: 2, z: 4, core: 2. Of those that a mesh axis runs over, the one named last changes fastest.
Arguments:
- tokens: bfloat16 [64, 256, 3584], P('rep', 'tp'), may hold values from -6 to 6
- seg_replica: int32 [32, 1], replicated, may hold values from 0 to 7; in each aligned block of 32 rows (0 to 31, 32 to 63, ...) at most 8 rows name the same one
- doc_of_segment: int32 [32], replicated, may hold values from 0 to 15, never falling along the last dimension, each value on 1 to 4 neighbouring positions
- doc_owner: int32 [16, 1], replicated, may hold values from 0 to 7; in each aligned block of 16 rows (0 to 15, 16 to 31, ...) at most 4 rows name the same one
- enc_gain: float32 [3584], replicated, may hold values from 0.5 to 1.5
- enc_query: bfloat16 [3584, 512], P(None, 'tp'), may hold values from -3.5 to 3.5
- enc_keyvalue: bfloat16 [3584, 2, 128], P(None, None, 'tp'), may hold values from -1 to 1
- enc_output: bfloat16 [512, 3584], P('tp'), may hold values from -0.25 to 0.25
- doc_proj: bfloat16 [3584, 256], P('tp'), may hold values from -0.09375 to 0.09375
- doc_gain: float32 [256], replicated, may hold values from 0.5 to 1.5
- doc_qkv: bfloat16 [256, 3, 256], P(None, None, 'tp'), may hold values from -4 to 4
Outputs:
- doc_context: bfloat16 [32, 4, 256], P('rep', None, 'tp')
The draws below stay inside these ranges and needn't reach their ends.
Inputs may be any that keep to these rules, and one draw needn't show every extreme that they name: `seg_replica`: no replica is assigned more than 8 segments, one replica exactly 8, every replica at least one. `doc_of_segment`: Non-decreasing; every document has 1 to 4 consecutive segments, some document exactly 4. `doc_owner`: no replica owns more than 4 documents, one exactly 4, every replica at least one.
All inputs are finite; a program needn't handle non-finite values.
Results may differ from the reference program's by a relative error of at most 0.014.
Values may be sent and summed in bfloat16 or wider, within the bound.
No kernel may reach another device: no remote copies, remote signals or barrier semaphores. Data moves between devices by JAX's collectives and lax.ppermute only.
A program may use at most 64 MiB of HBM per device.

```python
import math
import jax
import jax.numpy as jnp
import numpy as np
from jax import lax

D = 3584
HEAD_DIM = 128
HEADS = 4
KV_HEADS = 1
SEG_LEN = 256
CAP = 8
SEGS = 32
DOCS = 16
DOC_MOST = 4
OWN_DOCS = 4
DOC_HEAD = 64
DOC_HEADS = 4
DW = 256
N_REP = 8


def replicated_key_rows(key):
    base = jax.random.truncated_normal(key, -6.0, 6.0, (D, KV_HEADS * HEAD_DIM), jnp.float32)
    return base * D ** (-0.5)


def draw_enc_keyvalue(key, part):
    key_base = replicated_key_rows(key)
    key = jax.random.fold_in(key, 11)
    value_part = jax.random.truncated_normal(key, -6.0, 6.0, (D, KV_HEADS * HEAD_DIM), jnp.float32) * D ** (-0.5)
    joined = jnp.stack([key_base, value_part], axis=1)
    return jnp.clip(joined, -1.0, 1.0).astype(jnp.bfloat16)


def draw_enc_query(key, part):
    key = jax.random.fold_in(key, 12)
    fresh = jax.random.truncated_normal(key, -6.0, 6.0, (D, HEADS * HEAD_DIM), jnp.float32) * D ** (-0.5)
    result = fresh
    return jnp.clip(result, -3.5, 3.5).astype(jnp.bfloat16)


def draw_doc_qkv(key, part):
    key = jax.random.fold_in(key, 21)
    key_one, second_random_key, key_three = jax.random.split(key, 3)
    scale = DW ** (-0.5)
    key_base = jax.random.truncated_normal(key_one, -6.0, 6.0, (DW, DW), jnp.float32) * scale
    value_part = jax.random.truncated_normal(second_random_key, -6.0, 6.0, (DW, DW), jnp.float32) * scale
    fresh = jax.random.truncated_normal(key_three, -6.0, 6.0, (DW, DW), jnp.float32) * scale
    query_part = fresh
    joined = jnp.stack([query_part, key_base, value_part], axis=1)
    return jnp.clip(joined, -4.0, 4.0).astype(jnp.bfloat16)


def shard_levels(own_key, shape, cuts, smallest, high):
    level = 1.0
    for axis_at, blocks in cuts:
        draws = jax.random.uniform(jax.random.fold_in(jax.random.fold_in(own_key, 6), axis_at), (blocks,), jnp.float32, smallest / len(cuts), high / len(cuts))
        level = level * jnp.repeat(jnp.exp(draws), shape[axis_at] // blocks).reshape((-1,) + (1,) * (len(shape) - 1 - axis_at))
    return level


def profile(count, total, limit, skew):
    loads = [(1 << 20) // math.isqrt(rank ** skew) + 1 for rank in range(2, count + 1)]
    spare, counts = total - limit - (count - 1), [1] * (count - 1)
    while spare > 0:
        candidates = [i for i in range(count - 1) if counts[i] < limit]
        whole, left = sum([loads[i] for i in candidates]), spare
        for i in candidates:
            addition = min(limit - counts[i], max(1, left * loads[i] // whole), spare)
            counts[i] = counts[i] + addition
            spare = spare - addition
    return np.array([limit] + counts)


def ragged_sizes(own_key, count, total, limit, skew):
    if count == 2:
        one = jax.random.randint(own_key, (), max(1, total - limit), min(limit, total - 1) + 1)
        return jnp.stack([one, total - one])
    tallies = jnp.asarray(profile(count, total, limit, skew), jnp.int32)
    couples = (count - 1) // 2
    donor, sink = tallies[1:1 + 2 * couples:2], tallies[2:2 + 2 * couples:2]
    margin = jnp.minimum(donor - 1, limit - sink)
    passed = jax.random.randint(jax.random.fold_in(own_key, 1), (couples,), 0, 1 << 20) % (margin + 1)
    tallies = tallies.at[1:1 + 2 * couples:2].set(donor - passed).at[2:2 + 2 * couples:2].set(sink + passed)
    return tallies[jax.random.permutation(jax.random.fold_in(own_key, 2), count)]


def assign_block(own_key, own, number, rows, count, top, bound, slope):
    order = jax.random.permutation(own_key, count)
    heavy_load, usual = shares(count, rows * top, bound, slope, True), shares(count, rows * top, bound, slope, False)
    places = jnp.arange(count)

    def named(lengths, offset_by):
        used = int((lengths > 0).sum())
        fixed = max(1, used // 4)
        moved = fixed + (places - fixed + offset_by * (used - fixed)) % max(1, count - fixed)
        return jnp.zeros((count,), jnp.int32).at[order[jnp.where(places < fixed, places, moved)]].set(jnp.asarray(lengths, jnp.int32))

    lengths = jnp.where(number % 4 == 0, named(heavy_load, number // 4), named(usual, number - number // 4 - 1))
    mixed = jax.random.permutation(jax.random.fold_in(own, 3), count)
    donor, sink = mixed[0:count // 2 * 2:2], mixed[1:count // 2 * 2:2]
    room = jnp.minimum(lengths[donor] - 1, bound - lengths[sink]) // 2
    room = jnp.where((donor == order[0]) | (sink == order[0]) | (lengths[sink] == 0), 0, jnp.maximum(room, 0))
    moved = jax.random.randint(jax.random.fold_in(own, 4), (count // 2,), 0, 1 << 20) % (room + 1)
    lengths = lengths.at[donor].add(-moved).at[sink].add(moved)
    members = jnp.searchsorted(jnp.cumsum(lengths), jnp.arange(rows * top), side="right").astype(jnp.int32)
    table = members.reshape(top, rows).T
    table = table[jax.random.permutation(jax.random.fold_in(own, 1), rows)]
    offset_by = jax.random.randint(jax.random.fold_in(own, 2), (rows, 1), 0, top)
    return jnp.take_along_axis(table, (jnp.arange(top)[None, :] + offset_by) % top, axis=1)


def shares(amount, total, most, skew, full):
    weights = [(1 << 20) // math.isqrt(standing ** skew) + 1 for standing in range(1, amount + 1)]
    largest = most if full else min(most, max(-(-total // amount), total * weights[0] // sum(weights)))
    least = 1 if total - largest >= amount - 1 else 0
    given, spare = [largest] + [least] * (amount - 1), total - largest - least * (amount - 1)
    while spare > 0:
        candidates = [i for i in range(1, amount) if given[i] < largest] or [i for i in range(1, amount) if given[i] < most]
        whole, budget = sum([weights[i] for i in candidates]), spare
        for i in candidates:
            addition = min(most - given[i], max(1, budget * weights[i] // whole), spare)
            given[i] = given[i] + addition
            spare = spare - addition
    return np.array(given)


def normal_values(own_key, extent, width, bound, shards=(), held_as=jnp.bfloat16):
    values = width * jax.random.normal(own_key, extent, jnp.float32)
    if shards:
        values = values * shard_levels(own_key, extent, shards, -0.22, 0.18)
    return jnp.clip(values, -bound, bound).astype(held_as)


def setup_inputs(seed: int = 0) -> dict:
    keys = jax.random.split(jax.random.key(seed), 12)
    tokens = normal_values(keys[0], (N_REP * CAP, SEG_LEN, D), 1.0, 6.0, ((0, 8), (1, 4)))
    seg_replica_keys = jax.random.split(jax.random.fold_in(keys[1], 1), SEGS // SEGS)
    seg_replica_turns = jax.random.permutation(jax.random.fold_in(keys[1], 3), SEGS // SEGS)
    seg_replica = jax.vmap(lambda own, number: assign_block(jax.random.fold_in(keys[1], 2), own, number, SEGS, N_REP, 1, CAP, 2))(seg_replica_keys, seg_replica_turns).reshape((SEGS, 1))
    doc_of_segment = jnp.searchsorted(jnp.cumsum(ragged_sizes(keys[2], DOCS, SEGS, DOC_MOST, 1)), jnp.arange(SEGS), side="right").astype(jnp.int32)
    doc_owner_keys = jax.random.split(jax.random.fold_in(keys[3], 1), DOCS // DOCS)
    doc_owner_turns = jax.random.permutation(jax.random.fold_in(keys[3], 3), DOCS // DOCS)
    doc_owner = jax.vmap(lambda own, number: assign_block(jax.random.fold_in(keys[3], 2), own, number, DOCS, N_REP, 1, OWN_DOCS, 1))(doc_owner_keys, doc_owner_turns).reshape((DOCS, 1))
    enc_gain = jnp.clip(1.0 + 0.1 * jax.random.normal(keys[4], (D,), jnp.float32), 0.5, 1.5)
    enc_query = draw_enc_query(jax.random.fold_in(keys[11], 71), 0)
    enc_keyvalue = draw_enc_keyvalue(jax.random.fold_in(keys[11], 71), 0)
    enc_output = normal_values(keys[7], (HEADS * HEAD_DIM, D), (HEADS * HEAD_DIM) ** -0.5, 0.25, ((0, 4),))
    doc_proj = normal_values(keys[8], (D, DW), D ** -0.5, 0.09375, ((0, 4),))
    doc_gain = jnp.clip(1.0 + 0.1 * jax.random.normal(keys[9], (DW,), jnp.float32), 0.5, 1.5)
    doc_qkv = draw_doc_qkv(jax.random.fold_in(keys[11], 71), 0)
    return dict(tokens=tokens, seg_replica=seg_replica, doc_of_segment=doc_of_segment, doc_owner=doc_owner, enc_gain=enc_gain, enc_query=enc_query, enc_keyvalue=enc_keyvalue, enc_output=enc_output, doc_proj=doc_proj, doc_gain=doc_gain, doc_qkv=doc_qkv)


def slot_table(seg_replica):
    replica_of = seg_replica[:, 0]
    order = jnp.arange(replica_of.shape[0], dtype=jnp.int32)
    earlier = (replica_of[None, :] == replica_of[:, None]) & (order[None, :] < order[:, None])
    return replica_of * CAP + lax.optimization_barrier(jnp.sum(earlier.astype(jnp.int32), axis=1))

def owner_rows(doc_of_segment, doc_owner):
    owner_of = doc_owner[:, 0]
    doc_ids = jnp.arange(owner_of.shape[0], dtype=jnp.int32)
    earlier = (owner_of[None, :] == owner_of[:, None]) & (doc_ids[None, :] < doc_ids[:, None])
    doc_rank = lax.optimization_barrier(jnp.sum(earlier.astype(jnp.int32), axis=1))
    start_of = lax.optimization_barrier(jnp.sum((doc_of_segment[None, :] < doc_ids[:, None]).astype(jnp.int32), axis=1))
    matches = doc_of_segment[:, None] == doc_ids[None, :]
    seg_owner = lax.optimization_barrier(jnp.sum(jnp.where(matches, owner_of[None, :], 0), axis=1))
    seg_rank = lax.optimization_barrier(jnp.sum(jnp.where(matches, doc_rank[None, :], 0), axis=1))
    seg_start = lax.optimization_barrier(jnp.sum(jnp.where(matches, start_of[None, :], 0), axis=1))
    position = jnp.arange(doc_of_segment.shape[0], dtype=jnp.int32) - seg_start
    return seg_owner * (OWN_DOCS * DOC_MOST) + seg_rank * DOC_MOST + position

def encode(seg_tokens, enc_gain, enc_query, enc_keyvalue, enc_output):
    raw_float = seg_tokens.astype(jnp.float32)
    normed = (raw_float * lax.rsqrt(lax.optimization_barrier(jnp.mean(raw_float * raw_float, axis=-1, keepdims=True)) + 1e-06) * enc_gain).astype(jnp.bfloat16)
    queries = jnp.dot(normed, enc_query, preferred_element_type=jnp.float32).astype(jnp.bfloat16)
    key_rows = jnp.dot(normed, enc_keyvalue[:, 0, :], preferred_element_type=jnp.float32).astype(jnp.bfloat16)
    value_rows = jnp.dot(normed, enc_keyvalue[:, 1, :], preferred_element_type=jnp.float32).astype(jnp.bfloat16)
    queries = queries.reshape(SEG_LEN, HEADS, HEAD_DIM)
    kv_group = HEADS // KV_HEADS
    key_rows = jnp.repeat(key_rows.reshape(SEG_LEN, KV_HEADS, HEAD_DIM), kv_group, axis=1)
    value_rows = jnp.repeat(value_rows.reshape(SEG_LEN, KV_HEADS, HEAD_DIM), kv_group, axis=1)
    scores = jnp.einsum('qhe,khe->hqk', queries.astype(jnp.float32), key_rows.astype(jnp.float32)) * HEAD_DIM ** (-0.5)
    attn_weights = jax.nn.softmax(scores, axis=-1).astype(jnp.bfloat16)
    context = jnp.einsum('hqk,khe->qhe', attn_weights.astype(jnp.float32), value_rows.astype(jnp.float32)).astype(jnp.bfloat16)
    context_mean = lax.optimization_barrier(jnp.mean(context.astype(jnp.float32).reshape(SEG_LEN, HEADS * HEAD_DIM), axis=0))
    pooled = lax.optimization_barrier(jnp.mean(raw_float, axis=0)) + jnp.dot(context_mean[None, :], enc_output.astype(jnp.float32), precision=lax.Precision.HIGHEST)[0]
    return pooled.astype(jnp.bfloat16)

def reference(tokens, seg_replica, doc_of_segment, doc_owner, enc_gain, enc_query, enc_keyvalue, enc_output, doc_proj, doc_gain, doc_qkv):
    global_slot = slot_table(seg_replica)

    def encode_slot(slot_index):
        seg_tokens = lax.dynamic_index_in_dim(tokens, slot_index, 0, keepdims=False)
        return encode(seg_tokens, enc_gain, enc_query, enc_keyvalue, enc_output)
    pooled = lax.map(encode_slot, global_slot)
    row_of = owner_rows(doc_of_segment, doc_owner)
    total_rows = N_REP * OWN_DOCS * DOC_MOST
    owner_input_rows = jnp.zeros((total_rows, D), jnp.bfloat16).at[row_of].set(pooled)
    filled = jnp.zeros((total_rows,), jnp.float32).at[row_of].set(1.0)
    doc_first = jnp.dot(owner_input_rows, doc_proj, preferred_element_type=jnp.float32)
    doc_normed = (doc_first * lax.rsqrt(lax.optimization_barrier(jnp.mean(doc_first * doc_first, axis=-1, keepdims=True)) + 1e-06) * doc_gain).astype(jnp.bfloat16)
    projected = jnp.einsum('rc,cte->tre', doc_normed.astype(jnp.float32), doc_qkv.astype(jnp.float32)).astype(jnp.bfloat16)
    slots_all = N_REP * OWN_DOCS
    shaped = projected.reshape(3, slots_all, DOC_MOST, DOC_HEADS, DOC_HEAD).astype(jnp.float32)
    scores = jnp.einsum('bqhe,bkhe->bhqk', shaped[0], shaped[1]) * DOC_HEAD ** (-0.5)
    filled_rows = filled.reshape(slots_all, DOC_MOST)
    diagonal_mask = jnp.eye(DOC_MOST, dtype=bool)
    allowed = (filled_rows[:, None, None, :] > 0.5) | diagonal_mask[None, None, :, :]
    scores = jnp.where(allowed, scores, -1e+30)
    attn_weights = jax.nn.softmax(scores, axis=-1).astype(jnp.bfloat16)
    context = jnp.einsum('bhqk,bkhe->bqhe', attn_weights.astype(jnp.float32), shaped[2])
    context = context * filled_rows[:, :, None, None]
    return context.reshape(slots_all, DOC_MOST, DW).astype(jnp.bfloat16)
```

```python
import functools

import jax
import jax.numpy as jnp
from jax import lax
from jax.experimental import pallas as pl
from jax.experimental.pallas import tpu as pltpu
from jax.sharding import PartitionSpec as P

CAP = 8
DOC_MOST = 4
OWN_DOCS = 4
F32 = jnp.float32
BF16 = jnp.bfloat16
HIGH = lax.Precision.HIGHEST


def flipped(block, axis, mask):
    count = lax.axis_size(axis)
    return lax.ppermute(block, axis, [(i, i ^ mask) for i in range(count)])


def masks_of(count):
    masks = [0]
    bit = count // 2
    while bit:
        masks = masks + [m | bit for m in masks]
        bit //= 2
    return masks


def tp_blocks(block, count):
    blocks = [block]
    bit = count // 2
    while bit:
        blocks = blocks + [flipped(b, "tp", bit) for b in blocks]
        bit //= 2
    return blocks


def slot_table(seg_replica):
    replica_of = seg_replica[:, 0]
    order = jnp.arange(replica_of.shape[0], dtype=jnp.int32)
    earlier = (replica_of[None, :] == replica_of[:, None]) & (order[None, :] < order[:, None])
    return replica_of, jnp.sum(earlier.astype(jnp.int32), axis=1)


def owner_rows(doc_of_segment, doc_owner):
    owner_of = doc_owner[:, 0]
    doc_ids = jnp.arange(owner_of.shape[0], dtype=jnp.int32)
    earlier = (owner_of[None, :] == owner_of[:, None]) & (doc_ids[None, :] < doc_ids[:, None])
    doc_rank = jnp.sum(earlier.astype(jnp.int32), axis=1)
    start_of = jnp.sum((doc_of_segment[None, :] < doc_ids[:, None]).astype(jnp.int32), axis=1)
    matches = doc_of_segment[:, None] == doc_ids[None, :]
    seg_owner = jnp.sum(jnp.where(matches, owner_of[None, :], 0), axis=1)
    seg_rank = jnp.sum(jnp.where(matches, doc_rank[None, :], 0), axis=1)
    seg_start = jnp.sum(jnp.where(matches, start_of[None, :], 0), axis=1)
    position = jnp.arange(doc_of_segment.shape[0], dtype=jnp.int32) - seg_start
    return seg_owner * (OWN_DOCS * DOC_MOST) + seg_rank * DOC_MOST + position


def attention_kernel(group, head_dim, length, q_ref, kv_ref, w2_ref, xp_ref, out_ref, ctx_ref):
    slots, tokens, width = q_ref.shape
    heads = width // head_dim
    kv_heads = heads // group
    for s in range(slots):
        q = q_ref[s]
        for g in range(kv_heads):
            rows = jnp.concatenate(
                [q[:, h * head_dim:(h + 1) * head_dim] for h in range(g * group, (g + 1) * group)], axis=0
            )
            keys = kv_ref[:, s, :, g * 2 * head_dim:(g * 2 + 1) * head_dim].reshape(-1, head_dim)
            values = kv_ref[:, s, :, (g * 2 + 1) * head_dim:(g * 2 + 2) * head_dim].reshape(-1, head_dim)
            scores = lax.dot_general(
                rows, keys, (((1,), (1,)), ((), ())), preferred_element_type=F32
            ) * head_dim ** (-0.5)
            e = jnp.exp(scores - jnp.max(scores, axis=1, keepdims=True))
            probs = e * (1.0 / jnp.sum(e, axis=1, keepdims=True))
            weight = jnp.sum(probs.reshape(group, tokens, -1), axis=1)
            context = jnp.dot(weight, values.astype(F32), preferred_element_type=F32, precision=HIGH)
            for j in range(group):
                h = g * group + j
                ctx_ref[s:s + 1, h * head_dim:(h + 1) * head_dim] = context[j:j + 1] * (1.0 / length)
    out_ref[...] = xp_ref[...] + jnp.dot(
        ctx_ref[...], w2_ref[...].astype(F32), preferred_element_type=F32, precision=HIGH
    )


def document_kernel(rows_ref, sel_ref, allow_ref, fill_ref, gain_ref, qkv_ref, out_ref):
    docs, most, head = out_ref.shape
    first = jnp.dot(sel_ref[...], rows_ref[...], preferred_element_type=F32, precision=HIGH)
    scale = lax.rsqrt(jnp.mean(first * first, axis=-1, keepdims=True) + 1e-06)
    normed = (first * scale * gain_ref[...]).astype(BF16)
    q, k, v = (
        jnp.dot(normed, qkv_ref[i], preferred_element_type=F32).astype(BF16) for i in range(3)
    )
    scores = lax.dot_general(
        q, k, (((1,), (1,)), ((), ())), preferred_element_type=F32
    ) * head ** (-0.5)
    scores = jnp.where(allow_ref[...] > 0.5, scores, -1e30)
    e = jnp.exp(scores - jnp.max(scores, axis=1, keepdims=True))
    probs = (e / jnp.sum(e, axis=1, keepdims=True)).astype(BF16)
    context = jnp.dot(probs, v, preferred_element_type=F32) * fill_ref[...]
    for d in range(docs):
        out_ref[d] = context[d * most:(d + 1) * most].astype(BF16)


def local(
    tokens,
    seg_replica,
    doc_of_segment,
    doc_owner,
    enc_gain,
    enc_query,
    enc_keyvalue,
    enc_output,
    doc_proj,
    doc_gain,
    doc_qkv,
):
    n_rep, n_tp = lax.axis_size("rep"), lax.axis_size("tp")
    rep_index = lax.axis_index("rep")
    tp_index = lax.axis_index("tp")
    slots, own_tokens, width = tokens.shape
    length = own_tokens * n_tp
    head_dim = enc_query.shape[1]
    kv_width = enc_keyvalue.shape[2]
    group = head_dim // kv_width
    block = doc_proj.shape[0]
    doc_width = doc_proj.shape[1]
    masks = masks_of(n_tp)

    kv_weights = enc_keyvalue.reshape(width, 2 * kv_width)
    kv_all = jnp.concatenate(tp_blocks(kv_weights, n_tp), axis=1)
    q_blocks = tp_blocks(enc_query, n_tp)

    raw = tokens.astype(F32)
    normed = (
        raw * lax.rsqrt(jnp.mean(raw * raw, axis=-1, keepdims=True) + 1e-06) * enc_gain
    ).astype(BF16).reshape(slots * own_tokens, width)

    kv = jnp.dot(normed, kv_all, preferred_element_type=F32).astype(BF16)
    column = jnp.arange(2 * kv_width * n_tp, dtype=jnp.int32)
    mask_of = jnp.array(masks, jnp.int32)[column // (2 * kv_width)]
    inner = column % (2 * kv_width)
    target = (
        (mask_of // group) * (2 * head_dim)
        + (inner // kv_width) * head_dim
        + ((tp_index ^ mask_of) % group) * kv_width
        + inner % kv_width
    )
    place = (target[:, None] == column[None, :]).astype(BF16)
    kv = jnp.dot(kv, place, preferred_element_type=F32).astype(BF16)
    kv = kv.reshape(slots, own_tokens, kv.shape[1])
    kv_tokens = jnp.stack(tp_blocks(kv, n_tp), axis=0)

    half = doc_width // 2
    parity = rep_index % 2
    proj_half = lax.dynamic_slice_in_dim(doc_proj, parity * half, half, axis=1)
    proj_blocks = tp_blocks(proj_half, n_tp)
    w2_half = jnp.zeros((head_dim, half), F32)
    for mask, part in zip(masks, proj_blocks):
        piece = lax.dynamic_slice_in_dim(enc_output, (tp_index ^ mask) * block, block, axis=1)
        w2_half = w2_half + jnp.dot(piece, part, preferred_element_type=F32)
    w2_half = w2_half.astype(BF16)
    w2_other = flipped(w2_half, "rep", 1)
    w2_own = jnp.concatenate(
        [jnp.where(parity == 0, w2_half, w2_other), jnp.where(parity == 0, w2_other, w2_half)], axis=1
    )
    w2 = jnp.concatenate(tp_blocks(w2_own, n_tp), axis=0)

    sums = jnp.sum(raw, axis=1) * (1.0 / length)
    mine = sums.reshape(slots, n_tp, block)
    bit = n_tp // 2
    while bit:
        low = lax.dynamic_slice_in_dim(mine, (tp_index // bit % 2) * bit, bit, axis=1)
        far = lax.dynamic_slice_in_dim(mine, (1 - tp_index // bit % 2) * bit, bit, axis=1)
        mine = low + flipped(far, "tp", bit)
        bit //= 2
    mean_part = jnp.dot(mine.reshape(slots, block), doc_proj.astype(F32), precision=HIGH)

    queries = jnp.concatenate(
        [jnp.dot(normed, w, preferred_element_type=F32).astype(BF16) for w in q_blocks], axis=1
    ).reshape(slots, own_tokens, head_dim * n_tp)

    part = pl.pallas_call(
        functools.partial(attention_kernel, group, head_dim, length),
        out_shape=jax.ShapeDtypeStruct((slots, doc_width), F32),
        scratch_shapes=[pltpu.VMEM((slots, head_dim * n_tp), F32)],
        compiler_params=pltpu.CompilerParams(vmem_limit_bytes=40 * 2**20),
    )(queries, kv_tokens, w2, mean_part)

    bit = 1
    while bit < n_tp:
        part = part + flipped(part, "tp", bit)
        bit *= 2
    bit = 1
    while bit < n_rep:
        part = jnp.concatenate([part, flipped(part, "rep", bit)], axis=0)
        bit *= 2

    replica_of, rank = slot_table(seg_replica)
    row_of = owner_rows(doc_of_segment, doc_owner)
    owned = OWN_DOCS * DOC_MOST
    wanted = rep_index * owned + jnp.arange(owned, dtype=jnp.int32)
    matches = (row_of[None, :] == wanted[:, None]).astype(F32)
    at_slot = (replica_of ^ rep_index) * CAP + rank
    holds = (at_slot[:, None] == jnp.arange(n_rep * CAP, dtype=jnp.int32)[None, :]).astype(F32)
    select = jnp.dot(matches, holds)
    filled = jnp.sum(matches, axis=1)
    row = jnp.arange(owned, dtype=jnp.int32)
    same_doc = row[:, None] // DOC_MOST == row[None, :] // DOC_MOST
    allowed = same_doc & ((filled[None, :] > 0.5) | (row[:, None] == row[None, :]))

    return pl.pallas_call(
        document_kernel,
        out_shape=jax.ShapeDtypeStruct((OWN_DOCS, DOC_MOST, doc_qkv.shape[2]), BF16),
    )(
        part,
        select,
        allowed.astype(F32),
        filled[:, None],
        doc_gain[None, :],
        jnp.transpose(doc_qkv, (1, 0, 2)),
    )


def solution(mesh):
    in_specs = (
        P("rep", "tp", None),
        P(),
        P(),
        P(),
        P(),
        P(None, "tp"),
        P(None, None, "tp"),
        P("tp", None),
        P("tp", None),
        P(),
        P(None, None, "tp"),
    )
    out_specs = P("rep", None, "tp")
    return jax.shard_map(local, mesh=mesh, in_specs=in_specs, out_specs=out_specs, check_vma=False)
```

```python
import functools

import jax
import jax.numpy as jnp
from jax import lax
from jax.experimental import pallas as pl
from jax.experimental.pallas import tpu as pltpu
from jax.sharding import PartitionSpec as P

CAP = 8
DOC_MOST = 4
OWN_DOCS = 4
F32 = jnp.float32
BF16 = jnp.bfloat16
HIGH = lax.Precision.HIGHEST
NT = (((1,), (1,)), ((), ()))


def flipped(block, axis, mask):
    count = lax.axis_size(axis)
    return lax.ppermute(block, axis, [(i, i ^ mask) for i in range(count)])


def after(value, earlier):
    return lax.optimization_barrier((value, earlier))[0]


def cut(array, at, size, axis):
    return lax.dynamic_slice_in_dim(array, at * size, size, axis=axis)


def ordered(own, other, bit, axis):
    first = jnp.where(bit == 0, own, other)
    second = jnp.where(bit == 0, other, own)
    return jnp.concatenate([first, second], axis=axis)


def slot_table(seg_replica):
    replica_of = seg_replica[:, 0]
    order = jnp.arange(replica_of.shape[0], dtype=jnp.int32)
    earlier = (replica_of[None, :] == replica_of[:, None]) & (order[None, :] < order[:, None])
    return replica_of, jnp.sum(earlier.astype(jnp.int32), axis=1)


def owner_rows(doc_of_segment, doc_owner):
    owner_of = doc_owner[:, 0]
    doc_ids = jnp.arange(owner_of.shape[0], dtype=jnp.int32)
    earlier = (owner_of[None, :] == owner_of[:, None]) & (doc_ids[None, :] < doc_ids[:, None])
    doc_rank = jnp.sum(earlier.astype(jnp.int32), axis=1)
    start_of = jnp.sum((doc_of_segment[None, :] < doc_ids[:, None]).astype(jnp.int32), axis=1)
    matches = doc_of_segment[:, None] == doc_ids[None, :]
    seg_owner = jnp.sum(jnp.where(matches, owner_of[None, :], 0), axis=1)
    seg_rank = jnp.sum(jnp.where(matches, doc_rank[None, :], 0), axis=1)
    seg_start = jnp.sum(jnp.where(matches, start_of[None, :], 0), axis=1)
    position = jnp.arange(doc_of_segment.shape[0], dtype=jnp.int32) - seg_start
    return seg_owner * (OWN_DOCS * DOC_MOST) + seg_rank * DOC_MOST + position


def norm_kernel(tokens_ref, gain_ref, normed_ref, sum_ref):
    x = tokens_ref[0].astype(F32)
    scale = lax.rsqrt(jnp.mean(x * x, axis=-1, keepdims=True) + 1e-06)
    normed_ref[0] = (x * scale * gain_ref[...]).astype(BF16)
    sum_ref[0] = jnp.sum(x, axis=0, keepdims=True)


def normalized(tokens, gain):
    slots, count, width = tokens.shape
    return pl.pallas_call(
        norm_kernel,
        grid=(slots,),
        in_specs=[
            pl.BlockSpec((1, count, width), lambda i: (i, 0, 0)),
            pl.BlockSpec((1, width), lambda i: (0, 0)),
        ],
        out_specs=[
            pl.BlockSpec((1, count, width), lambda i: (i, 0, 0)),
            pl.BlockSpec((1, 1, width), lambda i: (i, 0, 0)),
        ],
        out_shape=[
            jax.ShapeDtypeStruct((slots, count, width), BF16),
            jax.ShapeDtypeStruct((slots, 1, width), F32),
        ],
        cost_estimate=pl.CostEstimate(
            flops=8 * tokens.size, bytes_accessed=4 * tokens.size, transcendentals=0
        ),
    )(tokens, gain)


def attention_kernel(masks, group, slots, length, *refs):
    n = len(masks)
    q_refs, near_refs, far_refs, w2_refs = (refs[i * n:(i + 1) * n] for i in range(4))
    place_ref, xp_ref, out_ref, ctx_ref = refs[4 * n:]
    rows, head_dim = q_refs[0].shape
    tokens = rows // (2 * slots)
    groups = sorted({m // group for m in masks})
    for s in range(slots):
        spans = [slice((c * slots + s) * tokens, (c * slots + s + 1) * tokens) for c in range(2)]
        kv = jnp.concatenate(
            [
                jnp.dot(
                    jnp.concatenate([near[spans[c], :], far[spans[1 - c], :]], axis=1),
                    place_ref[p],
                    preferred_element_type=F32,
                ).astype(BF16)
                for p, (near, far) in enumerate(zip(near_refs, far_refs))
                for c in range(2)
            ],
            axis=0,
        )
        for g in groups:
            heads = [p for p in range(n) if masks[p] // group == g]
            q = jnp.concatenate([q_refs[p][span, :] for p in heads for span in spans], axis=0)
            keys = kv[:, g * 2 * head_dim:(g * 2 + 1) * head_dim]
            values = kv[:, (g * 2 + 1) * head_dim:(g * 2 + 2) * head_dim]
            scores = lax.dot_general(q, keys, NT, preferred_element_type=F32) * head_dim ** (-0.5)
            e = jnp.exp(scores - jnp.max(scores, axis=1, keepdims=True))
            probs = e * (1.0 / jnp.sum(e, axis=1, keepdims=True))
            weight = jnp.sum(probs.reshape(len(heads), 2 * tokens, -1), axis=1)
            context = jnp.dot(weight, values.astype(F32), preferred_element_type=F32, precision=HIGH)
            for j, p in enumerate(heads):
                ctx_ref[p, s:s + 1, :] = context[j:j + 1] * (1.0 / length)
    total = xp_ref[...]
    for p in range(n):
        total += lax.dot_general(
            ctx_ref[p], w2_refs[p][...].astype(F32), NT, preferred_element_type=F32, precision=HIGH
        )
    out_ref[...] = total


def document_kernel(rows_ref, sel_ref, allow_ref, fill_ref, gain_ref, qkv_ref, out_ref):
    docs, most, head = out_ref.shape
    first = jnp.dot(sel_ref[...], rows_ref[...], preferred_element_type=F32, precision=HIGH)
    scale = lax.rsqrt(jnp.mean(first * first, axis=-1, keepdims=True) + 1e-06)
    normed = (first * scale * gain_ref[...]).astype(BF16)
    q, k, v = (
        lax.dot_general(normed, qkv_ref[i], NT, preferred_element_type=F32).astype(BF16) for i in range(3)
    )
    scores = lax.dot_general(q, k, NT, preferred_element_type=F32) * head ** (-0.5)
    scores = jnp.where(allow_ref[...] > 0.5, scores, -1e30)
    e = jnp.exp(scores - jnp.max(scores, axis=1, keepdims=True))
    probs = (e / jnp.sum(e, axis=1, keepdims=True)).astype(BF16)
    context = jnp.dot(probs, v, preferred_element_type=F32) * fill_ref[...]
    for d in range(docs):
        out_ref[d] = context[d * most:(d + 1) * most].astype(BF16)


def local(
    tokens,
    seg_replica,
    doc_of_segment,
    doc_owner,
    enc_gain,
    enc_query,
    enc_keyvalue,
    enc_output,
    doc_proj,
    doc_gain,
    doc_qkv,
):
    n_rep, n_tp = lax.axis_size("rep"), lax.axis_size("tp")
    rep_index = lax.axis_index("rep")
    tp_index = lax.axis_index("tp")
    x_bit, z_bit = rep_index % 2, rep_index // 2 % 2
    slots, own_tokens, width = tokens.shape
    length = own_tokens * n_tp
    head_dim = enc_query.shape[1]
    kv_width = enc_keyvalue.shape[2]
    group = head_dim // kv_width
    block, doc_width = doc_proj.shape
    masks = list(range(0, n_tp, 2))

    tokens_far = flipped(tokens, "tp", 1)

    kv_rows = jnp.transpose(enc_keyvalue, (1, 2, 0))
    part_kv = kv_width // 2
    part_doc = doc_width // 4
    proj_rows = part_doc * block // width
    proj = cut(doc_proj, z_bit * 2 + x_bit, part_doc, 1).T
    proj = jnp.concatenate(
        [proj[i * proj_rows:(i + 1) * proj_rows] for i in range(width // block)], axis=1
    )
    opening = jnp.concatenate(
        [cut(kv_rows[0], x_bit, part_kv, 0), cut(kv_rows[1], z_bit, part_kv, 0), proj], axis=0
    )
    received = [flipped(opening, "tp", m) for m in masks[1:]]

    part_q = width // 4
    q_half = jnp.concatenate(
        [cut(enc_query[:2 * part_q], x_bit, part_q, 0), cut(enc_query[2 * part_q:], z_bit, part_q, 0)], axis=0
    )
    q_half = after(q_half, received[0])
    q_received = [flipped(q_half, "tp", m) for m in masks[1:]]

    near, sums = normalized(tokens, enc_gain[None, :])

    kv_parts = [kv_rows.reshape(2 * kv_width, width)]
    for r in received:
        kv_parts += [
            r[:part_kv],
            flipped(r[:part_kv], "rep", 1),
            r[part_kv:2 * part_kv],
            flipped(r[part_kv:2 * part_kv], "rep", 2),
        ]
    kv_weights = jnp.concatenate(kv_parts, axis=0)

    far, sums_far = normalized(tokens_far, enc_gain[None, :])
    rows = slots * own_tokens
    normed = jnp.concatenate([near.reshape(rows, width), far.reshape(rows, width)], axis=0)

    proj_near = [proj] + [r[2 * part_kv:] for r in received]
    proj_far = flipped(jnp.concatenate(proj_near, axis=0), "tp", 1)
    proj_all = proj_near + [proj_far[i * proj_rows:(i + 1) * proj_rows] for i in range(len(masks))]
    origin = masks + [m + 1 for m in masks]
    proj_all = jnp.concatenate(
        [
            jnp.concatenate([p[:, i * block:(i + 1) * block] for i in range(width // block)], axis=0)
            for p in proj_all
        ],
        axis=1,
    )
    output_all = jnp.concatenate([cut(enc_output, tp_index ^ m, block, 1) for m in origin], axis=1)
    w2 = lax.dot_general(proj_all, output_all, NT, preferred_element_type=F32).astype(BF16)
    w2 = ordered(w2, flipped(w2, "rep", 1), x_bit, 0)
    w2 = ordered(w2, flipped(w2, "rep", 2), z_bit, 0)

    kv = lax.dot_general(normed, kv_weights, NT, preferred_element_type=F32).astype(BF16)
    lanes = kv.shape[1]
    mean = ((sums + sums_far) * (1.0 / length)).reshape(slots, n_tp // 2, 2, block)
    mean = lax.dynamic_index_in_dim(mean, tp_index % 2, 2, keepdims=False)

    def mean_of(m):
        return lax.dynamic_index_in_dim(mean, (tp_index ^ m) // 2, 1, keepdims=False)

    kv_near, w2_near, mean_here = [kv], [w2], mean_of(0)
    for m in masks[1:]:
        there = mean_of(m)
        high = there.astype(BF16)
        low = (there - high.astype(F32)).astype(BF16)
        both = jnp.stack([high, low], axis=0)
        pad = -both.size % (lanes * 8)
        both_rows = jnp.pad(both.reshape(-1), (0, pad)).reshape(-1, lanes)
        w2_rows = w2.reshape(-1, lanes)
        packed = jnp.concatenate([kv, w2_rows, both_rows], axis=0)
        packed = flipped(packed, "tp", m)
        kv_near.append(packed[:kv.shape[0]])
        w2_near.append(packed[kv.shape[0]:kv.shape[0] + w2_rows.shape[0]].reshape(w2.shape))
        both = packed[kv.shape[0] + w2_rows.shape[0]:].reshape(-1)[:both.size].reshape(both.shape)
        mean_here = mean_here + (both[0].astype(F32) + both[1].astype(F32))
    kv_far = [flipped(k, "tp", 1) for k in kv_near]
    mean_part = jnp.dot(mean_here, doc_proj.astype(F32), precision=HIGH)

    count = 2 * lanes
    column = jnp.arange(count, dtype=jnp.int32)
    core = column // lanes
    mask_of = column % lanes // (2 * kv_width) * 2
    inner = column % (2 * kv_width)
    quarter = inner // part_kv
    turn = jnp.where(quarter < 2, x_bit, z_bit)
    swapped = quarter // 2 * 2 + (quarter % 2 ^ turn)
    inner = jnp.where(mask_of == 0, inner, swapped * part_kv + inner % part_kv)
    places = []
    for m in masks:
        target = (
            (mask_of ^ m) // group * (2 * head_dim)
            + inner // kv_width * head_dim
            + (tp_index ^ m ^ mask_of ^ core) % group * kv_width
            + inner % kv_width
        )
        places.append((target[:, None] == column[None, :]).astype(BF16))
    place = jnp.stack(places, axis=0)

    early = jnp.concatenate(
        [cut(normed[:, :2 * part_q], x_bit, part_q, 1), cut(normed[:, 2 * part_q:], z_bit, part_q, 1)], axis=1
    )
    late = jnp.concatenate(
        [cut(normed[:, :2 * part_q], 1 - x_bit, part_q, 1), cut(normed[:, 2 * part_q:], 1 - z_bit, part_q, 1)],
        axis=1,
    )
    queries = [jnp.dot(normed, enc_query, preferred_element_type=F32).astype(BF16)]
    for r in q_received:
        rest = jnp.concatenate(
            [flipped(r[:part_q], "rep", 1), flipped(r[part_q:], "rep", 2)], axis=0
        )
        total = jnp.dot(early, r, preferred_element_type=F32)
        total = total + jnp.dot(late, rest, preferred_element_type=F32)
        queries.append(total.astype(BF16))

    part = pl.pallas_call(
        functools.partial(attention_kernel, masks, group, slots, length),
        out_shape=jax.ShapeDtypeStruct((slots, doc_width), F32),
        scratch_shapes=[pltpu.VMEM((len(masks), slots, head_dim), F32)],
        compiler_params=pltpu.CompilerParams(vmem_limit_bytes=40 * 2**20),
    )(*queries, *kv_near, *kv_far, *w2_near, place, mean_part)

    bit = 1
    while bit < n_tp:
        part = part + flipped(part, "tp", bit)
        bit *= 2
    bit = 1
    while bit < n_rep:
        part = jnp.concatenate([part, flipped(part, "rep", bit)], axis=0)
        bit *= 2

    replica_of, rank = slot_table(seg_replica)
    row_of = owner_rows(doc_of_segment, doc_owner)
    owned = OWN_DOCS * DOC_MOST
    wanted = rep_index * owned + jnp.arange(owned, dtype=jnp.int32)
    matches = (row_of[None, :] == wanted[:, None]).astype(F32)
    at_slot = (replica_of ^ rep_index) * CAP + rank
    holds = (at_slot[:, None] == jnp.arange(n_rep * CAP, dtype=jnp.int32)[None, :]).astype(F32)
    select = jnp.dot(matches, holds)
    filled = jnp.sum(matches, axis=1)
    row = jnp.arange(owned, dtype=jnp.int32)
    same_doc = row[:, None] // DOC_MOST == row[None, :] // DOC_MOST
    allowed = same_doc & ((filled[None, :] > 0.5) | (row[:, None] == row[None, :]))

    return pl.pallas_call(
        document_kernel,
        out_shape=jax.ShapeDtypeStruct((OWN_DOCS, DOC_MOST, doc_qkv.shape[2]), BF16),
    )(
        part,
        select,
        allowed.astype(F32),
        filled[:, None],
        doc_gain[None, :],
        jnp.transpose(doc_qkv, (1, 2, 0)),
    )


def solution(mesh):
    in_specs = (
        P("rep", "tp", None),
        P(),
        P(),
        P(),
        P(),
        P(None, "tp"),
        P(None, None, "tp"),
        P("tp", None),
        P("tp", None),
        P(),
        P(None, None, "tp"),
    )
    out_specs = P("rep", None, "tp")
    return jax.shard_map(local, mesh=mesh, in_specs=in_specs, out_specs=out_specs, check_vma=False)
```

```python
import functools

import jax
import jax.numpy as jnp
from jax import lax
from jax.experimental import pallas as pl
from jax.experimental.pallas import tpu as pltpu
from jax.sharding import PartitionSpec as P

CAP = 8
DOC_MOST = 4
OWN_DOCS = 4
F32 = jnp.float32
BF16 = jnp.bfloat16
HIGH = lax.Precision.HIGHEST
VMEM = 48 * 2**20
NT = (((1,), (1,)), ((), ()))


def flipped(block, axis, mask):
    count = lax.axis_size(axis)
    return lax.ppermute(block, axis, [(i, i ^ mask) for i in range(count)])


def cut(array, at, size, axis):
    return lax.dynamic_slice_in_dim(array, at * size, size, axis=axis)


def slot_table(seg_replica):
    replica_of = seg_replica[:, 0]
    order = jnp.arange(replica_of.shape[0], dtype=jnp.int32)
    earlier = (replica_of[None, :] == replica_of[:, None]) & (order[None, :] < order[:, None])
    return replica_of, jnp.sum(earlier.astype(jnp.int32), axis=1)


def owner_rows(doc_of_segment, doc_owner):
    owner_of = doc_owner[:, 0]
    doc_ids = jnp.arange(owner_of.shape[0], dtype=jnp.int32)
    earlier = (owner_of[None, :] == owner_of[:, None]) & (doc_ids[None, :] < doc_ids[:, None])
    doc_rank = jnp.sum(earlier.astype(jnp.int32), axis=1)
    start_of = jnp.sum((doc_of_segment[None, :] < doc_ids[:, None]).astype(jnp.int32), axis=1)
    matches = doc_of_segment[:, None] == doc_ids[None, :]
    seg_owner = jnp.sum(jnp.where(matches, owner_of[None, :], 0), axis=1)
    seg_rank = jnp.sum(jnp.where(matches, doc_rank[None, :], 0), axis=1)
    seg_start = jnp.sum(jnp.where(matches, start_of[None, :], 0), axis=1)
    position = jnp.arange(doc_of_segment.shape[0], dtype=jnp.int32) - seg_start
    return seg_owner * (OWN_DOCS * DOC_MOST) + seg_rank * DOC_MOST + position


def lane_step(width):
    step = 512
    while width % step:
        step //= 2
    return step


def token_kernel(tokens_ref, query_ref, q_ref, scale_ref, sum_ref):
    slots, count, width = tokens_ref.shape
    head_dim = query_ref.shape[1]
    step = lane_step(width)
    for s in range(slots):
        squares = jnp.zeros((count, 128), F32)
        for at in range(0, width, step):
            x = tokens_ref[s, :, at:at + step].astype(F32)
            sum_ref[s:s + 1, at:at + step] = jnp.sum(x, axis=0, keepdims=True)
            x = x * x
            for i in range(0, step, 128):
                squares += x[:, i:i + 128]
        mean = jnp.sum(squares, axis=1, keepdims=True) * (1.0 / width)
        scale_ref[s * count:(s + 1) * count, :] = jnp.broadcast_to(
            lax.rsqrt(mean + 1e-06), (count, head_dim)
        )
    tokens = tokens_ref[...].reshape(slots * count, width)
    q = jnp.dot(tokens, query_ref[...], preferred_element_type=F32)
    q_ref[...] = (q * scale_ref[...]).astype(BF16)


def token_parts(tokens, query):
    slots, count, width = tokens.shape
    head_dim = query.shape[1]
    rows = slots * count
    return pl.pallas_call(
        token_kernel,
        out_shape=[
            jax.ShapeDtypeStruct((rows, head_dim), BF16),
            jax.ShapeDtypeStruct((rows, head_dim), F32),
            jax.ShapeDtypeStruct((slots, width), F32),
        ],
        compiler_params=pltpu.CompilerParams(vmem_limit_bytes=VMEM),
        cost_estimate=pl.CostEstimate(
            flops=2 * rows * width * head_dim, bytes_accessed=2 * rows * width, transcendentals=0
        ),
    )(tokens, query)


def keyvalue_kernel(near_ref, far_ref, near_scale_ref, far_scale_ref, *refs):
    weight_refs, kv_ref = refs[:-1], refs[-1]
    slots, count, width = near_ref.shape
    rows = slots * count
    weights = jnp.concatenate([w[...] for w in weight_refs], axis=0)
    for c, (x_ref, scale_ref) in enumerate(((near_ref, near_scale_ref), (far_ref, far_scale_ref))):
        kv = lax.dot_general(x_ref[...].reshape(rows, width), weights, NT, preferred_element_type=F32)
        kv_ref[c * rows:(c + 1) * rows, :] = (kv * scale_ref[:, :1]).astype(BF16)


def half_query(x_ref, b_ref, c_ref, turn):
    slots, count, width = x_ref.shape
    part = b_ref.shape[0]
    rep = lax.axis_index("rep")
    at_b = pl.multiple_of((lax.rem(rep, 2) ^ turn) * part, 128)
    at_c = pl.multiple_of((2 + (lax.rem(rep // 2, 2) ^ turn)) * part, 128)
    rows = slots * count
    total = jnp.dot(
        x_ref[:, :, pl.ds(at_b, part)].reshape(rows, part), b_ref[...], preferred_element_type=F32
    )
    return total + jnp.dot(
        x_ref[:, :, pl.ds(at_c, part)].reshape(rows, part), c_ref[...], preferred_element_type=F32
    )


def early_kernel(near_ref, far_ref, b_ref, c_ref, out_ref):
    rows = out_ref.shape[0] // 2
    out_ref[:rows, :] = half_query(near_ref, b_ref, c_ref, 0)
    out_ref[rows:, :] = half_query(far_ref, b_ref, c_ref, 0)


def product_kernel(masks, output_ref, *refs):
    proj_refs, out_ref = refs[:-1], refs[-1]
    total = jnp.zeros(out_ref.shape, F32)
    for mask, proj_ref in zip(masks, proj_refs):
        total += lax.dot_general(proj_ref[...], output_ref[mask], NT, preferred_element_type=F32)
    out_ref[...] = total.astype(BF16)


def split(value):
    high = value.astype(BF16)
    return jnp.concatenate([high, (value - high.astype(F32)).astype(BF16)], axis=0)


def joined(value):
    half = value.shape[0] // 2
    return value[:half] + value[half:]


def attention_kernel(masks, group, length, *refs):
    n = len(masks)
    at = iter(range(len(refs)))

    def take(count):
        return [refs[next(at)] for _ in range(count)]

    x_refs = take(2)
    scale_refs = take(2)
    query_ref, = take(1)
    early_refs, b_refs, c_refs = take(n - 1), take(n - 1), take(n - 1)
    near_refs, far_refs = take(n), take(n)
    w2_refs = [take(2) for _ in range(n)]
    place_ref, mean_ref, proj_ref, out_ref, q_ref, kv_ref, score_ref, weight_ref, ctx_ref, w2_ref = take(10)
    slots, tokens, _ = x_refs[0].shape
    head_dim = query_ref.shape[1]
    rows = slots * tokens
    groups = sorted({m // group for m in masks})
    heads_of = [[p for p in range(n) if masks[p] // group == g] for g in groups]
    in_group = len(heads_of[0])

    rep = lax.axis_index("rep")
    quarter = lax.rem(rep, 4)
    part = w2_ref.shape[1] // 4
    for p in range(n):
        for i in range(4):
            at_row = pl.multiple_of((quarter ^ i) * part, part)
            w2_ref[p, pl.ds(at_row, part), :] = w2_refs[p][i // 2][i % 2 * part:(i % 2 + 1) * part, :]

    for p in range(n):
        for c in range(2):
            mixed = jnp.concatenate(
                [
                    near_refs[p][c * rows:(c + 1) * rows, :],
                    far_refs[p][(1 - c) * rows:(2 - c) * rows, :],
                ],
                axis=1,
            )
            kv_ref[p, c * rows:(c + 1) * rows, :] = jnp.dot(
                mixed, place_ref[p], preferred_element_type=F32
            ).astype(BF16)
    q_ref[0] = query_ref[...]
    for p in range(1, n):
        for c in range(2):
            span = slice(c * rows, (c + 1) * rows)
            q = early_refs[p - 1][span, :] + half_query(x_refs[c], b_refs[p - 1], c_refs[p - 1], 1)
            q_ref[p, span, :] = (q * scale_refs[c][...]).astype(BF16)

    def spans(s):
        return [slice(c * rows + s * tokens, c * rows + (s + 1) * tokens) for c in range(2)]

    def columns(s, first):
        return jnp.concatenate(
            [kv_ref[p, span, first:first + head_dim] for p in range(n) for span in spans(s)], axis=0
        )

    for s in range(slots):
        for g, heads in enumerate(heads_of):
            q = jnp.concatenate([q_ref[p, span, :] for p in heads for span in spans(s)], axis=0)
            keys = columns(s, g * 2 * head_dim)
            score_ref[s, g] = lax.dot_general(q, keys, NT, preferred_element_type=F32)
    for s in range(slots):
        for g in range(len(groups)):
            scores = score_ref[s, g]
            top = jnp.max(scores, axis=1, keepdims=True)
            e = jnp.exp((scores - top) * head_dim ** (-0.5))
            probs = e * (1.0 / jnp.sum(e, axis=1, keepdims=True))
            weight_ref[s, g] = jnp.sum(probs.reshape(in_group, 2 * tokens, -1), axis=1)
    for s in range(slots):
        for g, heads in enumerate(heads_of):
            values = columns(s, (g * 2 + 1) * head_dim)
            context = joined(
                jnp.dot(split(weight_ref[s, g]), values, preferred_element_type=F32)
            ) * (1.0 / length)
            for j, p in enumerate(heads):
                ctx_ref[p, s:s + 1, :] = context[j:j + 1]
    total = joined(jnp.dot(split(mean_ref[...]), proj_ref[...], preferred_element_type=F32))
    for p in range(n):
        total += joined(
            lax.dot_general(split(ctx_ref[p]), w2_ref[p], NT, preferred_element_type=F32)
        )
    out_ref[...] = total


def document_kernel(rows_ref, sel_ref, allow_ref, fill_ref, gain_ref, qkv_ref, out_ref):
    docs, most, head = out_ref.shape
    first = jnp.dot(sel_ref[...], rows_ref[...], preferred_element_type=F32, precision=HIGH)
    scale = lax.rsqrt(jnp.mean(first * first, axis=-1, keepdims=True) + 1e-06)
    normed = (first * scale * gain_ref[...]).astype(BF16)
    q, k, v = (
        lax.dot_general(normed, qkv_ref[i], NT, preferred_element_type=F32).astype(BF16) for i in range(3)
    )
    scores = lax.dot_general(q, k, NT, preferred_element_type=F32) * head ** (-0.5)
    scores = jnp.where(allow_ref[...] > 0.5, scores, -1e30)
    e = jnp.exp(scores - jnp.max(scores, axis=1, keepdims=True))
    probs = (e / jnp.sum(e, axis=1, keepdims=True)).astype(BF16)
    context = jnp.dot(probs, v, preferred_element_type=F32) * fill_ref[...]
    for d in range(docs):
        out_ref[d] = context[d * most:(d + 1) * most].astype(BF16)


def local(
    tokens,
    seg_replica,
    doc_of_segment,
    doc_owner,
    enc_gain,
    enc_query,
    enc_keyvalue,
    enc_output,
    doc_proj,
    doc_gain,
    doc_qkv,
):
    n_rep, n_tp = lax.axis_size("rep"), lax.axis_size("tp")
    rep_index = lax.axis_index("rep")
    tp_index = lax.axis_index("tp")
    x_bit, z_bit = rep_index % 2, rep_index // 2 % 2
    slots, own_tokens, width = tokens.shape
    length = own_tokens * n_tp
    head_dim = enc_query.shape[1]
    kv_width = enc_keyvalue.shape[2]
    group = head_dim // kv_width
    block, doc_width = doc_proj.shape
    masks = list(range(0, n_tp, 2))

    kv_rows = (jnp.transpose(enc_keyvalue, (1, 2, 0)).astype(F32) * enc_gain).astype(BF16)
    query = (enc_query.astype(F32) * enc_gain[:, None]).astype(BF16)
    part_kv, part_q, part_doc = kv_width // 2, width // 4, doc_width // 4
    keys_y = [flipped(cut(kv_rows[0], x_bit, part_kv, 0), "tp", m) for m in masks[1:]]
    values_y = [flipped(cut(kv_rows[1], z_bit, part_kv, 0), "tp", m) for m in masks[1:]]
    tokens_far = flipped(tokens, "tp", 1)
    proj = cut(doc_proj, z_bit * 2 + x_bit, part_doc, 1).T
    proj_near = [proj] + [flipped(proj, "tp", m) for m in masks[1:]]
    b_y = [flipped(cut(query, x_bit, part_q, 0), "tp", m) for m in masks[1:]]
    c_y = [flipped(cut(query, 2 + z_bit, part_q, 0), "tp", m) for m in masks[1:]]

    q_near, scale_near, sums_near = token_parts(tokens, query)

    weights = [kv_rows.reshape(2 * kv_width, width)]
    for k, v in zip(keys_y, values_y):
        weights += [k, flipped(k, "rep", 1), v, flipped(v, "rep", 2)]
    q_far, scale_far, sums_far = token_parts(tokens_far, query)

    rows = slots * own_tokens
    lanes = 2 * kv_width * len(masks)
    kv = pl.pallas_call(
        keyvalue_kernel,
        out_shape=jax.ShapeDtypeStruct((2 * rows, lanes), BF16),
        compiler_params=pltpu.CompilerParams(vmem_limit_bytes=VMEM),
        cost_estimate=pl.CostEstimate(
            flops=4 * rows * width * lanes, bytes_accessed=4 * rows * width, transcendentals=0
        ),
    )(tokens, tokens_far, scale_near, scale_far, *weights)
    kv_near = [kv] + [flipped(kv, "tp", m) for m in masks[1:]]
    kv_far = [flipped(k, "tp", 1) for k in kv_near]

    proj_all = proj_near + [flipped(p, "tp", 1) for p in proj_near]
    origin = masks + [m + 1 for m in masks]
    output_blocks = jnp.stack([cut(enc_output, tp_index ^ m, block, 1) for m in range(n_tp)], axis=0)
    w2 = pl.pallas_call(
        functools.partial(product_kernel, origin),
        out_shape=jax.ShapeDtypeStruct((part_doc, head_dim), BF16),
        compiler_params=pltpu.CompilerParams(vmem_limit_bytes=VMEM),
    )(output_blocks, *proj_all)
    w2 = jnp.concatenate([w2, flipped(w2, "rep", 1)], axis=0)
    w2_pair = [w2, flipped(w2, "rep", 2)]
    w2_all = w2_pair + [flipped(w, "tp", m) for m in masks[1:] for w in w2_pair]

    mean = ((sums_near + sums_far) * (1.0 / length)).reshape(slots, n_tp, block)

    def mean_of(m):
        return lax.dynamic_index_in_dim(mean, tp_index ^ m, 1, keepdims=False)

    mean_here = mean_of(0)
    for m in masks[1:]:
        mean_here = mean_here + flipped(mean_of(m), "tp", m)

    count = 2 * lanes
    column = jnp.arange(count, dtype=jnp.int32)
    core = column // lanes
    mask_of = column % lanes // (2 * kv_width) * 2
    inner = column % (2 * kv_width)
    quarter = inner // part_kv
    turn = jnp.where(quarter < 2, x_bit, z_bit)
    swapped = quarter // 2 * 2 + (quarter % 2 ^ turn)
    inner = jnp.where(mask_of == 0, inner, swapped * part_kv + inner % part_kv)
    places = []
    for m in masks:
        target = (
            (mask_of ^ m) // group * (2 * head_dim)
            + inner // kv_width * head_dim
            + (tp_index ^ m ^ mask_of ^ core) % group * kv_width
            + inner % kv_width
        )
        places.append((target[:, None] == column[None, :]).astype(BF16))
    place = jnp.stack(places, axis=0)

    early, b_rest, c_rest = [], [], []
    for q_b, q_c in zip(b_y, c_y):
        b_rest.append(flipped(q_b, "rep", 1))
        c_rest.append(flipped(q_c, "rep", 2))
        early.append(
            pl.pallas_call(
                early_kernel,
                out_shape=jax.ShapeDtypeStruct((2 * rows, head_dim), F32),
                compiler_params=pltpu.CompilerParams(vmem_limit_bytes=VMEM),
                cost_estimate=pl.CostEstimate(
                    flops=2 * rows * width * head_dim, bytes_accessed=2 * rows * width, transcendentals=0
                ),
            )(tokens, tokens_far, q_b, q_c)
        )

    n = len(masks)
    groups = n_tp // group
    part = pl.pallas_call(
        functools.partial(attention_kernel, masks, group, length),
        out_shape=jax.ShapeDtypeStruct((slots, doc_width), F32),
        scratch_shapes=[
            pltpu.VMEM((n, 2 * rows, head_dim), BF16),
            pltpu.VMEM((n, 2 * rows, 2 * lanes), BF16),
            pltpu.VMEM((slots, groups, n // groups * 2 * own_tokens, length), F32),
            pltpu.VMEM((slots, groups, n // groups, length), F32),
            pltpu.VMEM((n, slots, head_dim), F32),
            pltpu.VMEM((n, doc_width, head_dim), BF16),
        ],
        compiler_params=pltpu.CompilerParams(vmem_limit_bytes=VMEM),
    )(
        tokens,
        tokens_far,
        scale_near,
        scale_far,
        jnp.concatenate([q_near, q_far], axis=0),
        *early,
        *b_rest,
        *c_rest,
        *kv_near,
        *kv_far,
        *w2_all,
        place,
        mean_here,
        doc_proj,
    )

    bit = 1
    while bit < n_tp:
        part = part + flipped(part, "tp", bit)
        bit *= 2
    bit = 1
    while bit < n_rep:
        part = jnp.concatenate([part, flipped(part, "rep", bit)], axis=0)
        bit *= 2

    replica_of, rank = slot_table(seg_replica)
    row_of = owner_rows(doc_of_segment, doc_owner)
    owned = OWN_DOCS * DOC_MOST
    wanted = rep_index * owned + jnp.arange(owned, dtype=jnp.int32)
    matches = (row_of[None, :] == wanted[:, None]).astype(F32)
    at_slot = (replica_of ^ rep_index) * CAP + rank
    holds = (at_slot[:, None] == jnp.arange(n_rep * CAP, dtype=jnp.int32)[None, :]).astype(F32)
    select = jnp.dot(matches, holds)
    filled = jnp.sum(matches, axis=1)
    row = jnp.arange(owned, dtype=jnp.int32)
    same_doc = row[:, None] // DOC_MOST == row[None, :] // DOC_MOST
    allowed = same_doc & ((filled[None, :] > 0.5) | (row[:, None] == row[None, :]))

    return pl.pallas_call(
        document_kernel,
        out_shape=jax.ShapeDtypeStruct((OWN_DOCS, DOC_MOST, doc_qkv.shape[2]), BF16),
    )(
        part,
        select,
        allowed.astype(F32),
        filled[:, None],
        doc_gain[None, :],
        jnp.transpose(doc_qkv, (1, 2, 0)),
    )


def solution(mesh):
    in_specs = (
        P("rep", "tp", None),
        P(),
        P(),
        P(),
        P(),
        P(None, "tp"),
        P(None, None, "tp"),
        P("tp", None),
        P("tp", None),
        P(),
        P(None, None, "tp"),
    )
    out_specs = P("rep", None, "tp")
    return jax.shard_map(local, mesh=mesh, in_specs=in_specs, out_specs=out_specs, check_vma=False)
```

```python
import functools
import math

import jax
import jax.numpy as jnp
from jax import lax
from jax.experimental import pallas as pl
from jax.experimental.pallas import tpu as pltpu
from jax.sharding import PartitionSpec as P

CAP = 8
DOC_MOST = 4
OWN_DOCS = 4
F32 = jnp.float32
BF16 = jnp.bfloat16
NT = (((1,), (1,)), ((), ()))


def flipped(block, axis, mask):
    count = lax.axis_size(axis)
    return lax.ppermute(block, axis, [(i, i ^ mask) for i in range(count)])


def after(value, earlier):
    return lax.optimization_barrier((value, earlier))[0]


def cut(array, at, size, axis):
    return lax.dynamic_slice_in_dim(array, at * size, size, axis=axis)


def slot_table(seg_replica):
    replica_of = seg_replica[:, 0]
    order = jnp.arange(replica_of.shape[0], dtype=jnp.int32)
    earlier = (replica_of[None, :] == replica_of[:, None]) & (order[None, :] < order[:, None])
    return replica_of, jnp.sum(earlier.astype(jnp.int32), axis=1)


def owner_rows(doc_of_segment, doc_owner):
    owner_of = doc_owner[:, 0]
    doc_ids = jnp.arange(owner_of.shape[0], dtype=jnp.int32)
    earlier = (owner_of[None, :] == owner_of[:, None]) & (doc_ids[None, :] < doc_ids[:, None])
    doc_rank = jnp.sum(earlier.astype(jnp.int32), axis=1)
    start_of = jnp.sum((doc_of_segment[None, :] < doc_ids[:, None]).astype(jnp.int32), axis=1)
    matches = doc_of_segment[:, None] == doc_ids[None, :]
    seg_owner = jnp.sum(jnp.where(matches, owner_of[None, :], 0), axis=1)
    seg_rank = jnp.sum(jnp.where(matches, doc_rank[None, :], 0), axis=1)
    seg_start = jnp.sum(jnp.where(matches, start_of[None, :], 0), axis=1)
    position = jnp.arange(doc_of_segment.shape[0], dtype=jnp.int32) - seg_start
    return seg_owner * (OWN_DOCS * DOC_MOST) + seg_rank * DOC_MOST + position


def room(*arrays):
    total = sum(math.prod(a.shape) * jnp.dtype(a.dtype).itemsize for a in arrays)
    return pltpu.CompilerParams(vmem_limit_bytes=total * 5 // 4 + 6 * 2**20)


def lane_step(width):
    step = 512
    while width % step:
        step //= 2
    return step


def parities():
    rep = lax.axis_index("rep")
    return lax.rem(rep, 2), lax.rem(rep // 2, 2)


def token_kernel(order_ref, x_ref, gain_ref, own_ref, scale_ref, sum_ref):
    slots, count, width = x_ref.shape
    step = lane_step(width)
    for s in range(slots):
        squares = jnp.zeros((count, 128), F32)
        for at in range(0, width, step):
            x = x_ref[s, :, at:at + step].astype(F32)
            sum_ref[s:s + 1, at:at + step] = jnp.sum(x, axis=0, keepdims=True)
            x = x * x
            for i in range(0, step, 128):
                squares += x[:, i:i + 128]
        mean = jnp.sum(squares, axis=1, keepdims=True) * (1.0 / width)
        scale_ref[s * count:(s + 1) * count, :] = jnp.broadcast_to(
            lax.rsqrt(mean + 1e-06), (count, scale_ref.shape[1])
        )


def keyvalue_kernel(length, near_ref, far_ref, gain_ref, own_ref, near_scale_ref, near_sum_ref, *refs):
    half_refs, (kv_ref, near_out, far_out, scale_ref, mean_ref) = refs[:-5], refs[-5:]
    slots, count, width = near_ref.shape
    rows = slots * count
    step = lane_step(width)
    parts = [own_ref[0], own_ref[1]]
    for here, there in zip(half_refs[::2], half_refs[1::2]):
        parts += [here[0], there[0], here[1], there[1]]
    weights = jnp.concatenate(parts, axis=0)
    scale_ref[:rows, :] = near_scale_ref[...]
    for c, (x_ref, out_ref) in enumerate(((near_ref, near_out), (far_ref, far_out))):
        for s in range(slots):
            squares = jnp.zeros((count, 128), F32)
            for at in range(0, width, step):
                x = x_ref[s, :, at:at + step].astype(F32)
                out_ref[s, :, at:at + step] = (x * gain_ref[at:at + step].reshape(1, step)).astype(BF16)
                if c:
                    total = jnp.sum(x, axis=0, keepdims=True) + near_sum_ref[s:s + 1, at:at + step]
                    mean_ref[s:s + 1, at:at + step] = total * (1.0 / length)
                    x = x * x
                    for i in range(0, step, 128):
                        squares += x[:, i:i + 128]
            if c:
                mean = jnp.sum(squares, axis=1, keepdims=True) * (1.0 / width)
                at_row = c * rows + s * count
                scale_ref[at_row:at_row + count, :] = jnp.broadcast_to(
                    lax.rsqrt(mean + 1e-06), (count, scale_ref.shape[1])
                )
        kv = lax.dot_general(out_ref[...].reshape(rows, width), weights, NT, preferred_element_type=F32)
        span = slice(c * rows, (c + 1) * rows)
        kv_ref[span, :] = (kv * scale_ref[span, :1]).astype(BF16)


def half_query(x_ref, b_ref, c_ref, turn):
    slots, count, width = x_ref.shape
    part = b_ref.shape[0]
    x_bit, z_bit = parities()
    at_b = pl.multiple_of((x_bit ^ turn) * part, 128)
    at_c = pl.multiple_of((2 + (z_bit ^ turn)) * part, 128)
    rows = slots * count
    total = jnp.dot(
        x_ref[:, :, pl.ds(at_b, part)].reshape(rows, part), b_ref[...], preferred_element_type=F32
    )
    return total + jnp.dot(
        x_ref[:, :, pl.ds(at_c, part)].reshape(rows, part), c_ref[...], preferred_element_type=F32
    )


def query_kernel(near_ref, far_ref, scale_ref, query_ref, *refs):
    part_refs, (own_ref, *half_refs) = refs[:len(refs) // 3 * 2], refs[len(refs) // 3 * 2:]
    slots, count, width = near_ref.shape
    rows = slots * count
    for c, x_ref in enumerate((near_ref, far_ref)):
        span = slice(c * rows, (c + 1) * rows)
        for p, half_ref in enumerate(half_refs):
            half_ref[span, :] = half_query(x_ref, part_refs[2 * p], part_refs[2 * p + 1], 0)
        q = jnp.dot(x_ref[...].reshape(rows, width), query_ref[...], preferred_element_type=F32)
        own_ref[span, :] = (q * scale_ref[span, :]).astype(BF16)


def product_kernel(masks, order_ref, output_ref, *refs):
    proj_refs, out_ref = refs[:-1], refs[-1]
    total = jnp.zeros(out_ref.shape, F32)
    for mask, proj_ref in zip(masks, proj_refs):
        total += jnp.dot(output_ref[mask], proj_ref[...], preferred_element_type=F32)
    out_ref[...] = total.astype(BF16)


def split(value):
    high = value.astype(BF16)
    return jnp.concatenate([high, (value - high.astype(F32)).astype(BF16)], axis=0)


def joined(value):
    half = value.shape[0] // 2
    return value[:half] + value[half:]


def attention_kernel(masks, group, length, *refs):
    n = len(masks)
    at = iter(range(len(refs)))

    def take(count):
        return [refs[next(at)] for _ in range(count)]

    x_refs = take(2)
    scale_ref, query_ref = take(2)
    early_refs, b_refs, c_refs = take(n - 1), take(n - 1), take(n - 1)
    near_refs, far_refs = take(n), take(n)
    w2_refs = [take(2) for _ in range(n)]
    mean_refs = take(n)
    place_ref, proj_ref, out_ref, q_ref, kv_ref, score_ref, weight_ref, ctx_ref, w2_ref = take(9)
    slots, tokens, _ = x_refs[0].shape
    head_dim = query_ref.shape[1]
    rows = slots * tokens
    groups = sorted({m // group for m in masks})
    heads_of = [[p for p in range(n) if masks[p] // group == g] for g in groups]
    in_group = len(heads_of[0])

    x_bit, _ = parities()
    part = w2_ref.shape[2] // 2
    for p in range(n):
        for i in range(2):
            at_lane = pl.multiple_of((x_bit ^ i) * part, 128)
            w2_ref[p, :, pl.ds(at_lane, part)] = w2_refs[p][i][...]

    for p in range(n):
        for c in range(2):
            mixed = jnp.concatenate(
                [
                    near_refs[p][c * rows:(c + 1) * rows, :],
                    far_refs[p][(1 - c) * rows:(2 - c) * rows, :],
                ],
                axis=1,
            )
            kv_ref[p, c * rows:(c + 1) * rows, :] = jnp.dot(
                mixed, place_ref[p], preferred_element_type=F32
            ).astype(BF16)
    q_ref[0] = query_ref[...]
    for p in range(1, n):
        for c in range(2):
            span = slice(c * rows, (c + 1) * rows)
            q = early_refs[p - 1][span, :] + half_query(x_refs[c], b_refs[p - 1], c_refs[p - 1], 1)
            q_ref[p, span, :] = (q * scale_ref[span, :]).astype(BF16)

    def spans(s):
        return [slice(c * rows + s * tokens, c * rows + (s + 1) * tokens) for c in range(2)]

    def columns(s, first):
        return jnp.concatenate(
            [kv_ref[p, span, first:first + head_dim] for p in range(n) for span in spans(s)], axis=0
        )

    for s in range(slots):
        for g, heads in enumerate(heads_of):
            q = jnp.concatenate([q_ref[p, span, :] for p in heads for span in spans(s)], axis=0)
            keys = columns(s, g * 2 * head_dim)
            score_ref[s, g] = lax.dot_general(q, keys, NT, preferred_element_type=F32)
    for s in range(slots):
        for g in range(len(groups)):
            scores = score_ref[s, g]
            top = jnp.max(scores, axis=1, keepdims=True)
            e = jnp.exp((scores - top) * head_dim ** (-0.5))
            probs = e * (1.0 / jnp.sum(e, axis=1, keepdims=True))
            weight_ref[s, g] = jnp.sum(probs.reshape(in_group, 2 * tokens, -1), axis=1)
    for s in range(slots):
        for g, heads in enumerate(heads_of):
            values = columns(s, (g * 2 + 1) * head_dim)
            context = joined(
                jnp.dot(split(weight_ref[s, g]), values, preferred_element_type=F32)
            ) * (1.0 / length)
            for j, p in enumerate(heads):
                ctx_ref[p, s:s + 1, :] = context[j:j + 1]
    mean = mean_refs[0][...]
    for p in range(1, n):
        mean += mean_refs[p][...]
    total = joined(jnp.dot(split(mean), proj_ref[...], preferred_element_type=F32))
    for p in range(n):
        total += joined(jnp.dot(split(ctx_ref[p]), w2_ref[p], preferred_element_type=F32))
    out_ref[...] = total


def document_kernel(near_ref, far_ref, select_ref, allow_ref, fill_ref, gain_ref, qkv_ref, out_ref):
    docs, most, head = out_ref.shape
    rows = jnp.concatenate([near_ref[...], far_ref[...]], axis=0)
    high = rows.astype(BF16)
    rest = rows - high.astype(F32)
    middle = rest.astype(BF16)
    low = (rest - middle.astype(F32)).astype(BF16)
    select = select_ref[...].astype(BF16)
    first = sum(jnp.dot(select, part, preferred_element_type=F32) for part in (high, middle, low))
    scale = lax.rsqrt(jnp.mean(first * first, axis=-1, keepdims=True) + 1e-06)
    normed = (first * scale * gain_ref[...]).astype(BF16)
    q, k, v = (
        lax.dot_general(normed, qkv_ref[i], NT, preferred_element_type=F32).astype(BF16) for i in range(3)
    )
    scores = lax.dot_general(q, k, NT, preferred_element_type=F32) * head ** (-0.5)
    scores = jnp.where(allow_ref[...] > 0.5, scores, -1e30)
    e = jnp.exp(scores - jnp.max(scores, axis=1, keepdims=True))
    probs = (e / jnp.sum(e, axis=1, keepdims=True)).astype(BF16)
    context = jnp.dot(probs, v, preferred_element_type=F32) * fill_ref[...]
    for d in range(docs):
        out_ref[d] = context[d * most:(d + 1) * most].astype(BF16)


def local(
    tokens,
    seg_replica,
    doc_of_segment,
    doc_owner,
    enc_gain,
    enc_query,
    enc_keyvalue,
    enc_output,
    doc_proj,
    doc_gain,
    doc_qkv,
):
    n_rep, n_tp = lax.axis_size("rep"), lax.axis_size("tp")
    rep_index = lax.axis_index("rep")
    tp_index = lax.axis_index("tp")
    x_bit, z_bit = rep_index % 2, rep_index // 2 % 2
    slots, own_tokens, width = tokens.shape
    length = own_tokens * n_tp
    head_dim = enc_query.shape[1]
    kv_width = enc_keyvalue.shape[2]
    group = head_dim // kv_width
    block, doc_width = doc_proj.shape
    masks = list(range(0, n_tp, 2))

    kv_rows = jnp.transpose(enc_keyvalue, (1, 2, 0))
    kv_half = cut(kv_rows, x_bit, kv_width // 2, 1)
    kv_y = [flipped(kv_half, "tp", m) for m in masks[1:]]
    tokens_far = flipped(tokens, "tp", 1)
    part_q, part_doc = width // 4, doc_width // 2
    query_here = after(enc_query, kv_half)
    b_part, c_part = cut(query_here, x_bit, part_q, 0), cut(query_here, 2 + z_bit, part_q, 0)
    b_y = [flipped(b_part, "tp", m) for m in masks[1:]]
    c_y = [flipped(c_part, "tp", m) for m in masks[1:]]
    proj = cut(after(doc_proj, (b_part, c_part)), x_bit, part_doc, 1)
    proj_near = [proj] + [flipped(proj, "tp", m) for m in masks[1:]]

    weights = []
    for w in kv_y:
        weights += [w, flipped(w, "rep", 1)]

    rows = slots * own_tokens
    lanes = 2 * kv_width * len(masks)
    out = [
        jax.ShapeDtypeStruct((rows, head_dim), F32),
        jax.ShapeDtypeStruct((slots, width), F32),
    ]
    scale, sums = pl.pallas_call(
        token_kernel,
        in_specs=[pl.BlockSpec(memory_space=pl.ANY)] + [pl.BlockSpec(memory_space=pltpu.VMEM)] * 3,
        out_shape=out,
        compiler_params=room(tokens, enc_gain, kv_rows, *out),
    )(kv_y[0], tokens, enc_gain, kv_rows)
    operands = (tokens, tokens_far, enc_gain, kv_rows, scale, sums, *weights)
    out = [
        jax.ShapeDtypeStruct((2 * rows, lanes), BF16),
        jax.ShapeDtypeStruct(tokens.shape, BF16),
        jax.ShapeDtypeStruct(tokens.shape, BF16),
        jax.ShapeDtypeStruct((2 * rows, head_dim), F32),
        jax.ShapeDtypeStruct((slots, width), F32),
    ]
    kv, near, far, scale, mean = pl.pallas_call(
        functools.partial(keyvalue_kernel, length),
        out_shape=out,
        compiler_params=room(*operands, *out),
    )(*operands)
    kv_near = [kv] + [flipped(kv, "tp", m) for m in masks[1:]]
    kv_far = [flipped(k, "tp", 1) for k in kv_near]

    proj_near = [after(p, kv) for p in proj_near]
    proj_all = proj_near + [flipped(p, "tp", 1) for p in proj_near]
    origin = masks + [m + 1 for m in masks]
    output_blocks = jnp.stack([cut(after(enc_output, kv), tp_index ^ m, block, 1) for m in range(n_tp)], axis=0)
    out = jax.ShapeDtypeStruct((head_dim, part_doc), BF16)
    w2 = pl.pallas_call(
        functools.partial(product_kernel, origin),
        in_specs=[pl.BlockSpec(memory_space=pl.ANY)]
        + [pl.BlockSpec(memory_space=pltpu.VMEM)] * (1 + n_tp),
        out_shape=out,
        compiler_params=room(output_blocks, *proj_all, out),
    )(kv, output_blocks, *proj_all)
    w2_pair = [w2, flipped(w2, "rep", 1)]
    count = 2 * lanes
    column = jnp.arange(count, dtype=jnp.int32)
    core = column // lanes
    mask_of = column % lanes // (2 * kv_width) * 2
    inner = column % (2 * kv_width)
    part_kv = kv_width // 2
    quarter = inner // part_kv
    swapped = quarter // 2 * 2 + (quarter % 2 ^ x_bit)
    inner = jnp.where(mask_of == 0, inner, swapped * part_kv + inner % part_kv)
    places = []
    for m in masks:
        target = (
            (mask_of ^ m) // group * (2 * head_dim)
            + inner // kv_width * head_dim
            + (tp_index ^ m ^ mask_of ^ core) % group * kv_width
            + inner % kv_width
        )
        places.append((target[:, None] == column[None, :]).astype(BF16))
    place = jnp.stack(places, axis=0)

    parts, b_rest, c_rest = [], [], []
    for q_b, q_c in zip(b_y, c_y):
        q_b, q_c = after((q_b, q_c), kv)
        parts += [q_b, q_c]
        b_rest.append(flipped(q_b, "rep", 1))
        c_rest.append(flipped(q_c, "rep", 2))
    operands = (near, far, scale, enc_query, *parts)
    out = [jax.ShapeDtypeStruct((2 * rows, head_dim), BF16)]
    out += [jax.ShapeDtypeStruct((2 * rows, head_dim), F32) for _ in masks[1:]]
    own, *early = pl.pallas_call(
        query_kernel, out_shape=out, compiler_params=room(*operands, *out)
    )(*operands)

    mean, *w2_pair = after((mean, *w2_pair), own)
    mean = mean.reshape(slots, n_tp, block)

    def mean_of(m):
        return lax.dynamic_index_in_dim(mean, tp_index ^ m, 1, keepdims=False)

    means = [mean_of(0)] + [flipped(mean_of(m), "tp", m) for m in masks[1:]]
    w2_all = w2_pair + [flipped(w, "tp", m) for m in masks[1:] for w in w2_pair]

    n = len(masks)
    groups = n_tp // group
    operands = (
        near,
        far,
        scale,
        own,
        *early,
        *b_rest,
        *c_rest,
        *kv_near,
        *kv_far,
        *w2_all,
        *means,
        place,
        doc_proj,
    )
    scratch = [
        pltpu.VMEM((n, 2 * rows, head_dim), BF16),
        pltpu.VMEM((n, 2 * rows, 2 * lanes), BF16),
        pltpu.VMEM((slots, groups, n // groups * 2 * own_tokens, length), F32),
        pltpu.VMEM((slots, groups, n // groups, length), F32),
        pltpu.VMEM((n, slots, head_dim), F32),
        pltpu.VMEM((n, head_dim, doc_width), BF16),
    ]
    part = pl.pallas_call(
        functools.partial(attention_kernel, masks, group, length),
        out_shape=jax.ShapeDtypeStruct((slots, doc_width), F32),
        scratch_shapes=scratch,
        compiler_params=room(*operands, *scratch),
    )(*operands)

    bit = 1
    while bit < n_tp:
        part = part + flipped(part, "tp", bit)
        bit *= 2
    bit = 1
    while bit < n_rep // 2:
        part = jnp.concatenate([part, flipped(part, "rep", bit)], axis=0)
        bit *= 2
    part_far = flipped(part, "rep", bit)

    seg_replica, doc_of_segment, doc_owner = after((seg_replica, doc_of_segment, doc_owner), kv)
    replica_of, rank = slot_table(seg_replica)
    row_of = owner_rows(doc_of_segment, doc_owner)
    owned = OWN_DOCS * DOC_MOST
    wanted = rep_index * owned + jnp.arange(owned, dtype=jnp.int32)
    matches = (row_of[None, :] == wanted[:, None]).astype(F32)
    at_slot = (replica_of ^ rep_index) * CAP + rank
    holds = (at_slot[:, None] == jnp.arange(n_rep * CAP, dtype=jnp.int32)[None, :]).astype(F32)
    select = jnp.dot(matches, holds)
    filled = jnp.sum(matches, axis=1)
    row = jnp.arange(owned, dtype=jnp.int32)
    same_doc = row[:, None] // DOC_MOST == row[None, :] // DOC_MOST
    allowed = same_doc & ((filled[None, :] > 0.5) | (row[:, None] == row[None, :]))

    operands = (
        part,
        part_far,
        select,
        allowed.astype(F32),
        filled[:, None],
        doc_gain[None, :],
        jnp.transpose(doc_qkv, (1, 2, 0)),
    )
    return pl.pallas_call(
        document_kernel,
        out_shape=jax.ShapeDtypeStruct((OWN_DOCS, DOC_MOST, doc_qkv.shape[2]), BF16),
        compiler_params=room(*operands),
    )(*operands)


def solution(mesh):
    in_specs = (
        P("rep", "tp", None),
        P(),
        P(),
        P(),
        P(),
        P(None, "tp"),
        P(None, None, "tp"),
        P("tp", None),
        P("tp", None),
        P(),
        P(None, None, "tp"),
    )
    out_specs = P("rep", None, "tp")
    return jax.shard_map(local, mesh=mesh, in_specs=in_specs, out_specs=out_specs, check_vma=False)
```

```python
import functools
import math

import jax
import jax.numpy as jnp
from jax import lax
from jax.experimental import pallas as pl
from jax.experimental.pallas import tpu as pltpu
from jax.sharding import PartitionSpec as P

CAP = 8
DOC_MOST = 4
OWN_DOCS = 4
F32 = jnp.float32
BF16 = jnp.bfloat16
NT = (((1,), (1,)), ((), ()))


def flipped(block, axis, mask):
    count = lax.axis_size(axis)
    return lax.ppermute(block, axis, [(i, i ^ mask) for i in range(count)])


def after(value, earlier):
    return lax.optimization_barrier((value, earlier))[0]


def cut(array, at, size, axis):
    return lax.dynamic_slice_in_dim(array, at * size, size, axis=axis)


def slot_table(seg_replica):
    replica_of = seg_replica[:, 0]
    order = jnp.arange(replica_of.shape[0], dtype=jnp.int32)
    earlier = (replica_of[None, :] == replica_of[:, None]) & (order[None, :] < order[:, None])
    return replica_of, jnp.sum(earlier.astype(jnp.int32), axis=1)


def owner_rows(doc_of_segment, doc_owner):
    owner_of = doc_owner[:, 0]
    doc_ids = jnp.arange(owner_of.shape[0], dtype=jnp.int32)
    earlier = (owner_of[None, :] == owner_of[:, None]) & (doc_ids[None, :] < doc_ids[:, None])
    doc_rank = jnp.sum(earlier.astype(jnp.int32), axis=1)
    start_of = jnp.sum((doc_of_segment[None, :] < doc_ids[:, None]).astype(jnp.int32), axis=1)
    matches = doc_of_segment[:, None] == doc_ids[None, :]
    seg_owner = jnp.sum(jnp.where(matches, owner_of[None, :], 0), axis=1)
    seg_rank = jnp.sum(jnp.where(matches, doc_rank[None, :], 0), axis=1)
    seg_start = jnp.sum(jnp.where(matches, start_of[None, :], 0), axis=1)
    position = jnp.arange(doc_of_segment.shape[0], dtype=jnp.int32) - seg_start
    return seg_owner * (OWN_DOCS * DOC_MOST) + seg_rank * DOC_MOST + position


def room(*arrays):
    total = sum(math.prod(a.shape) * jnp.dtype(a.dtype).itemsize for a in arrays)
    return pltpu.CompilerParams(vmem_limit_bytes=total * 5 // 4 + 6 * 2**20)


def lane_step(width):
    step = 512
    while width % step:
        step //= 2
    return step


def parities():
    rep = lax.axis_index("rep")
    return lax.rem(rep, 2), lax.rem(rep // 2, 2)


def token_kernel(order_ref, x_ref, gain_ref, own_ref, scale_ref, sum_ref):
    slots, count, width = x_ref.shape
    step = lane_step(width)
    for s in range(slots):
        squares = jnp.zeros((count, 128), F32)
        for at in range(0, width, step):
            x = x_ref[s, :, at:at + step].astype(F32)
            sum_ref[s:s + 1, at:at + step] = jnp.sum(x, axis=0, keepdims=True)
            x = x * x
            for i in range(0, step, 128):
                squares += x[:, i:i + 128]
        mean = jnp.sum(squares, axis=1, keepdims=True) * (1.0 / width)
        scale_ref[s * count:(s + 1) * count, :] = jnp.broadcast_to(
            lax.rsqrt(mean + 1e-06), (count, scale_ref.shape[1])
        )


def keyvalue_kernel(length, near_ref, far_ref, gain_ref, own_ref, near_scale_ref, near_sum_ref, *refs):
    half_refs, (kv_ref, near_out, far_out, scale_ref, mean_ref) = refs[:-5], refs[-5:]
    slots, count, width = near_ref.shape
    rows = slots * count
    step = lane_step(width)
    parts = [own_ref[0], own_ref[1]]
    for here, there in zip(half_refs[::2], half_refs[1::2]):
        parts += [here[0], there[0], here[1], there[1]]
    weights = jnp.concatenate(parts, axis=0)
    scale_ref[:rows, :] = near_scale_ref[...]
    for c, (x_ref, out_ref) in enumerate(((near_ref, near_out), (far_ref, far_out))):
        for s in range(slots):
            squares = jnp.zeros((count, 128), F32)
            for at in range(0, width, step):
                x = x_ref[s, :, at:at + step].astype(F32)
                out_ref[s, :, at:at + step] = (x * gain_ref[at:at + step].reshape(1, step)).astype(BF16)
                if c:
                    total = jnp.sum(x, axis=0, keepdims=True) + near_sum_ref[s:s + 1, at:at + step]
                    mean_ref[s:s + 1, at:at + step] = total * (1.0 / length)
                    x = x * x
                    for i in range(0, step, 128):
                        squares += x[:, i:i + 128]
            if c:
                mean = jnp.sum(squares, axis=1, keepdims=True) * (1.0 / width)
                at_row = c * rows + s * count
                scale_ref[at_row:at_row + count, :] = jnp.broadcast_to(
                    lax.rsqrt(mean + 1e-06), (count, scale_ref.shape[1])
                )
        kv = lax.dot_general(out_ref[...].reshape(rows, width), weights, NT, preferred_element_type=F32)
        span = slice(c * rows, (c + 1) * rows)
        kv_ref[span, :] = (kv * scale_ref[span, :1]).astype(BF16)


def half_query(x_ref, b_ref, c_ref, turn):
    slots, count, width = x_ref.shape
    part = b_ref.shape[0]
    x_bit, z_bit = parities()
    at_b = pl.multiple_of((x_bit ^ turn) * part, 128)
    at_c = pl.multiple_of((2 + (z_bit ^ turn)) * part, 128)
    rows = slots * count
    total = jnp.dot(
        x_ref[:, :, pl.ds(at_b, part)].reshape(rows, part), b_ref[...], preferred_element_type=F32
    )
    return total + jnp.dot(
        x_ref[:, :, pl.ds(at_c, part)].reshape(rows, part), c_ref[...], preferred_element_type=F32
    )


def query_kernel(order_ref, near_ref, far_ref, scale_ref, query_ref, *refs):
    part_refs, (own_ref, *half_refs) = refs[:len(refs) // 3 * 2], refs[len(refs) // 3 * 2:]
    slots, count, width = near_ref.shape
    rows = slots * count
    for c, x_ref in enumerate((near_ref, far_ref)):
        span = slice(c * rows, (c + 1) * rows)
        for p, half_ref in enumerate(half_refs):
            half_ref[span, :] = half_query(x_ref, part_refs[2 * p], part_refs[2 * p + 1], 0)
        q = jnp.dot(x_ref[...].reshape(rows, width), query_ref[...], preferred_element_type=F32)
        own_ref[span, :] = (q * scale_ref[span, :]).astype(BF16)


def product_kernel(masks, order_ref, output_ref, *refs):
    n = len(masks)
    proj_refs, mean_refs, (out_ref, *packed_refs) = refs[:n], refs[n:n * 3 // 2 - 1], refs[n * 3 // 2 - 1:]
    total = jnp.zeros(out_ref.shape, F32)
    for mask, proj_ref in zip(masks, proj_refs):
        total += jnp.dot(output_ref[mask], proj_ref[...], preferred_element_type=F32)
    out_ref[...] = total.astype(BF16)
    height, lanes = out_ref.shape
    for mean_ref, packed_ref in zip(mean_refs, packed_refs):
        packed_ref[:height, :] = total.astype(BF16)
        both = split(mean_ref[...])
        rows, block = both.shape
        for i in range(0, block, lanes):
            take = min(lanes, block - i)
            at = height + i // lanes * rows
            if take < lanes:
                packed_ref[at:at + rows, :] = jnp.zeros((rows, lanes), BF16)
            packed_ref[at:at + rows, :take] = both[:, i:i + take]


def split(value):
    high = value.astype(BF16)
    return jnp.concatenate([high, (value - high.astype(F32)).astype(BF16)], axis=0)


def joined(value):
    half = value.shape[0] // 2
    return value[:half] + value[half:]


def attention_kernel(masks, group, length, *refs):
    n = len(masks)
    at = iter(range(len(refs)))

    def take(count):
        return [refs[next(at)] for _ in range(count)]

    x_refs = take(2)
    scale_ref, query_ref = take(2)
    early_refs, b_refs, c_refs = take(n - 1), take(n - 1), take(n - 1)
    near_refs, far_refs = take(n), take(n)
    w2_refs = [take(2) for _ in range(n)]
    mean_ref, = take(1)
    place_ref, proj_ref, out_ref, q_ref, kv_ref, score_ref, weight_ref, ctx_ref, w2_ref = take(9)
    slots, tokens, _ = x_refs[0].shape
    head_dim = query_ref.shape[1]
    rows = slots * tokens
    groups = sorted({m // group for m in masks})
    heads_of = [[p for p in range(n) if masks[p] // group == g] for g in groups]
    in_group = len(heads_of[0])

    x_bit, _ = parities()
    part = w2_ref.shape[2] // 2
    for p in range(n):
        for i in range(2):
            at_lane = pl.multiple_of((x_bit ^ i) * part, 128)
            w2_ref[p, :, pl.ds(at_lane, part)] = w2_refs[p][i][:head_dim, :]

    for p in range(n):
        for c in range(2):
            mixed = jnp.concatenate(
                [
                    near_refs[p][c * rows:(c + 1) * rows, :],
                    far_refs[p][(1 - c) * rows:(2 - c) * rows, :],
                ],
                axis=1,
            )
            kv_ref[p, c * rows:(c + 1) * rows, :] = jnp.dot(
                mixed, place_ref[p], preferred_element_type=F32
            ).astype(BF16)
    q_ref[0] = query_ref[...]
    for p in range(1, n):
        for c in range(2):
            span = slice(c * rows, (c + 1) * rows)
            q = early_refs[p - 1][span, :] + half_query(x_refs[c], b_refs[p - 1], c_refs[p - 1], 1)
            q_ref[p, span, :] = (q * scale_ref[span, :]).astype(BF16)

    def spans(s):
        return [slice(c * rows + s * tokens, c * rows + (s + 1) * tokens) for c in range(2)]

    def columns(s, first):
        return jnp.concatenate(
            [kv_ref[p, span, first:first + head_dim] for p in range(n) for span in spans(s)], axis=0
        )

    for s in range(slots):
        for g, heads in enumerate(heads_of):
            q = jnp.concatenate([q_ref[p, span, :] for p in heads for span in spans(s)], axis=0)
            keys = columns(s, g * 2 * head_dim)
            score_ref[s, g] = lax.dot_general(q, keys, NT, preferred_element_type=F32)
    for s in range(slots):
        for g in range(len(groups)):
            scores = score_ref[s, g]
            top = jnp.max(scores, axis=1, keepdims=True)
            e = jnp.exp((scores - top) * head_dim ** (-0.5))
            probs = e * (1.0 / jnp.sum(e, axis=1, keepdims=True))
            weight_ref[s, g] = jnp.sum(probs.reshape(in_group, 2 * tokens, -1), axis=1)
    for s in range(slots):
        for g, heads in enumerate(heads_of):
            values = columns(s, (g * 2 + 1) * head_dim)
            context = joined(
                jnp.dot(split(weight_ref[s, g]), values, preferred_element_type=F32)
            ) * (1.0 / length)
            for j, p in enumerate(heads):
                ctx_ref[p, s:s + 1, :] = context[j:j + 1]
    mean = mean_ref[...]
    for p in range(1, n):
        packed = w2_refs[p][0]
        chunks = [
            packed[at:at + 2 * slots, :] for at in range(head_dim, packed.shape[0], 2 * slots)
        ]
        both = jnp.concatenate(chunks, axis=1)[:, :mean.shape[1]]
        mean += joined(both.astype(F32))
    total = joined(jnp.dot(split(mean), proj_ref[...], preferred_element_type=F32))
    for p in range(n):
        total += joined(jnp.dot(split(ctx_ref[p]), w2_ref[p], preferred_element_type=F32))
    out_ref[...] = total


def document_kernel(near_ref, far_ref, select_ref, allow_ref, fill_ref, gain_ref, qkv_ref, out_ref):
    docs, most, head = out_ref.shape
    rows = jnp.concatenate([near_ref[...], far_ref[...]], axis=0)
    high = rows.astype(BF16)
    rest = rows - high.astype(F32)
    middle = rest.astype(BF16)
    low = (rest - middle.astype(F32)).astype(BF16)
    select = select_ref[...].astype(BF16)
    first = sum(jnp.dot(select, part, preferred_element_type=F32) for part in (high, middle, low))
    scale = lax.rsqrt(jnp.mean(first * first, axis=-1, keepdims=True) + 1e-06)
    normed = (first * scale * gain_ref[...]).astype(BF16)
    q, k, v = (
        lax.dot_general(normed, qkv_ref[i], NT, preferred_element_type=F32).astype(BF16) for i in range(3)
    )
    scores = lax.dot_general(q, k, NT, preferred_element_type=F32) * head ** (-0.5)
    scores = jnp.where(allow_ref[...] > 0.5, scores, -1e30)
    e = jnp.exp(scores - jnp.max(scores, axis=1, keepdims=True))
    probs = (e / jnp.sum(e, axis=1, keepdims=True)).astype(BF16)
    context = jnp.dot(probs, v, preferred_element_type=F32) * fill_ref[...]
    for d in range(docs):
        out_ref[d] = context[d * most:(d + 1) * most].astype(BF16)


def local(
    tokens,
    seg_replica,
    doc_of_segment,
    doc_owner,
    enc_gain,
    enc_query,
    enc_keyvalue,
    enc_output,
    doc_proj,
    doc_gain,
    doc_qkv,
):
    n_rep, n_tp = lax.axis_size("rep"), lax.axis_size("tp")
    rep_index = lax.axis_index("rep")
    tp_index = lax.axis_index("tp")
    x_bit, z_bit = rep_index % 2, rep_index // 2 % 2
    slots, own_tokens, width = tokens.shape
    length = own_tokens * n_tp
    head_dim = enc_query.shape[1]
    kv_width = enc_keyvalue.shape[2]
    group = head_dim // kv_width
    block, doc_width = doc_proj.shape
    masks = list(range(0, n_tp, 2))

    kv_rows = jnp.transpose(enc_keyvalue, (1, 2, 0))
    kv_half = cut(kv_rows, x_bit, kv_width // 2, 1)
    kv_y = [flipped(kv_half, "tp", m) for m in masks[1:]]
    tokens_far = flipped(tokens, "tp", 1)
    part_q, part_doc = width // 4, doc_width // 2
    proj = cut(after(doc_proj, kv_half), x_bit, part_doc, 1)
    proj_near = [proj] + [flipped(proj, "tp", m) for m in masks[1:]]
    query_here = after(enc_query, proj)
    b_part, c_part = cut(query_here, x_bit, part_q, 0), cut(query_here, 2 + z_bit, part_q, 0)
    b_y = [flipped(b_part, "tp", m) for m in masks[1:]]
    c_y = [flipped(c_part, "tp", m) for m in masks[1:]]

    weights = []
    for w in kv_y:
        weights += [w, flipped(w, "rep", 1)]

    rows = slots * own_tokens
    lanes = 2 * kv_width * len(masks)
    out = [
        jax.ShapeDtypeStruct((rows, head_dim), F32),
        jax.ShapeDtypeStruct((slots, width), F32),
    ]
    scale, sums = pl.pallas_call(
        token_kernel,
        in_specs=[pl.BlockSpec(memory_space=pl.ANY)] + [pl.BlockSpec(memory_space=pltpu.VMEM)] * 3,
        out_shape=out,
        compiler_params=room(tokens, enc_gain, kv_rows, *out),
    )(kv_y[0], tokens, enc_gain, kv_rows)
    operands = (tokens, tokens_far, enc_gain, kv_rows, scale, sums, *weights)
    out = [
        jax.ShapeDtypeStruct((2 * rows, lanes), BF16),
        jax.ShapeDtypeStruct(tokens.shape, BF16),
        jax.ShapeDtypeStruct(tokens.shape, BF16),
        jax.ShapeDtypeStruct((2 * rows, head_dim), F32),
        jax.ShapeDtypeStruct((slots, width), F32),
    ]
    kv, near, far, scale, mean = pl.pallas_call(
        functools.partial(keyvalue_kernel, length),
        out_shape=out,
        compiler_params=room(*operands, *out),
    )(*operands)
    kv_near = [kv] + [flipped(kv, "tp", m) for m in masks[1:]]
    kv_far = [flipped(after(k, kv_near[1:]), "tp", 1) for k in kv_near]

    proj_near = [after(p, weights[-1]) for p in proj_near]
    proj_all = proj_near + [flipped(p, "tp", 1) for p in proj_near]
    origin = masks + [m + 1 for m in masks]
    output_blocks = jnp.stack([cut(after(enc_output, weights[-1]), tp_index ^ m, block, 1) for m in range(n_tp)], axis=0)
    mean = mean.reshape(slots, n_tp, block)
    means = [lax.dynamic_index_in_dim(mean, tp_index ^ m, 1, keepdims=False) for m in masks]
    height = head_dim + -(-block // part_doc) * 2 * slots
    out = [jax.ShapeDtypeStruct((head_dim, part_doc), BF16)]
    out += [jax.ShapeDtypeStruct((height, part_doc), BF16) for _ in masks[1:]]
    w2, *packed = pl.pallas_call(
        functools.partial(product_kernel, origin),
        in_specs=[pl.BlockSpec(memory_space=pl.ANY)]
        + [pl.BlockSpec(memory_space=pltpu.VMEM)] * (n_tp + len(masks)),
        out_shape=out,
        compiler_params=room(output_blocks, *proj_all, *means, *out),
    )(kv, output_blocks, *proj_all, *means[1:])
    w2_all = [w2, flipped(w2, "rep", 1)]
    for m, p in zip(masks[1:], packed):
        w2_all += [flipped(p, "tp", m), flipped(w2_all[1], "tp", m)]

    count = 2 * lanes
    column = jnp.arange(count, dtype=jnp.int32)
    core = column // lanes
    mask_of = column % lanes // (2 * kv_width) * 2
    inner = column % (2 * kv_width)
    part_kv = kv_width // 2
    quarter = inner // part_kv
    swapped = quarter // 2 * 2 + (quarter % 2 ^ x_bit)
    inner = jnp.where(mask_of == 0, inner, swapped * part_kv + inner % part_kv)
    places = []
    for m in masks:
        target = (
            (mask_of ^ m) // group * (2 * head_dim)
            + inner // kv_width * head_dim
            + (tp_index ^ m ^ mask_of ^ core) % group * kv_width
            + inner % kv_width
        )
        places.append((target[:, None] == column[None, :]).astype(BF16))
    place = jnp.stack(places, axis=0)

    parts, b_rest, c_rest = [], [], []
    for q_b, q_c in zip(b_y, c_y):
        q_b, q_c = after((q_b, q_c), kv)
        parts += [q_b, q_c]
        b_rest.append(flipped(q_b, "rep", 1))
        c_rest.append(flipped(q_c, "rep", 2))
    operands = (near, far, scale, enc_query, *parts)
    out = [jax.ShapeDtypeStruct((2 * rows, head_dim), BF16)]
    out += [jax.ShapeDtypeStruct((2 * rows, head_dim), F32) for _ in masks[1:]]
    own, *early = pl.pallas_call(
        query_kernel,
        in_specs=[pl.BlockSpec(memory_space=pl.ANY)]
        + [pl.BlockSpec(memory_space=pltpu.VMEM)] * len(operands),
        out_shape=out,
        compiler_params=room(*operands, *out),
    )(w2_all[1], *operands)

    n = len(masks)
    groups = n_tp // group
    operands = (
        near,
        far,
        scale,
        own,
        *early,
        *b_rest,
        *c_rest,
        *kv_near,
        *kv_far,
        *w2_all,
        means[0],
        place,
        doc_proj,
    )
    scratch = [
        pltpu.VMEM((n, 2 * rows, head_dim), BF16),
        pltpu.VMEM((n, 2 * rows, 2 * lanes), BF16),
        pltpu.VMEM((slots, groups, n // groups * 2 * own_tokens, length), F32),
        pltpu.VMEM((slots, groups, n // groups, length), F32),
        pltpu.VMEM((n, slots, head_dim), F32),
        pltpu.VMEM((n, head_dim, doc_width), BF16),
    ]
    part = pl.pallas_call(
        functools.partial(attention_kernel, masks, group, length),
        out_shape=jax.ShapeDtypeStruct((slots, doc_width), F32),
        scratch_shapes=scratch,
        compiler_params=room(*operands, *scratch),
    )(*operands)

    part = part + flipped(part, "tp", 1) + flipped(part, "tp", 2) + flipped(part, "tp", 3)
    bit = 4
    while bit < n_tp:
        part = part + flipped(part, "tp", bit)
        bit *= 2
    bit = 1
    while bit < n_rep // 2:
        part = jnp.concatenate([part, flipped(part, "rep", bit)], axis=0)
        bit *= 2
    part_far = flipped(part, "rep", bit)

    seg_replica, doc_of_segment, doc_owner = after((seg_replica, doc_of_segment, doc_owner), kv)
    replica_of, rank = slot_table(seg_replica)
    row_of = owner_rows(doc_of_segment, doc_owner)
    owned = OWN_DOCS * DOC_MOST
    wanted = rep_index * owned + jnp.arange(owned, dtype=jnp.int32)
    matches = (row_of[None, :] == wanted[:, None]).astype(F32)
    at_slot = (replica_of ^ rep_index) * CAP + rank
    holds = (at_slot[:, None] == jnp.arange(n_rep * CAP, dtype=jnp.int32)[None, :]).astype(F32)
    select = jnp.dot(matches, holds)
    filled = jnp.sum(matches, axis=1)
    row = jnp.arange(owned, dtype=jnp.int32)
    same_doc = row[:, None] // DOC_MOST == row[None, :] // DOC_MOST
    allowed = same_doc & ((filled[None, :] > 0.5) | (row[:, None] == row[None, :]))

    operands = (
        part,
        part_far,
        select,
        allowed.astype(F32),
        filled[:, None],
        doc_gain[None, :],
        jnp.transpose(doc_qkv, (1, 2, 0)),
    )
    return pl.pallas_call(
        document_kernel,
        out_shape=jax.ShapeDtypeStruct((OWN_DOCS, DOC_MOST, doc_qkv.shape[2]), BF16),
        compiler_params=room(*operands),
    )(*operands)


def solution(mesh):
    in_specs = (
        P("rep", "tp", None),
        P(),
        P(),
        P(),
        P(),
        P(None, "tp"),
        P(None, None, "tp"),
        P("tp", None),
        P("tp", None),
        P(),
        P(None, None, "tp"),
    )
    out_specs = P("rep", None, "tp")
    return jax.shard_map(local, mesh=mesh, in_specs=in_specs, out_specs=out_specs, check_vma=False)
```

```python
import functools
import math

import jax
import jax.numpy as jnp
from jax import lax
from jax.experimental import pallas as pl
from jax.experimental.pallas import tpu as pltpu
from jax.sharding import PartitionSpec as P

CAP = 8
DOC_MOST = 4
OWN_DOCS = 4
F32 = jnp.float32
BF16 = jnp.bfloat16
NT = (((1,), (1,)), ((), ()))


def flipped(block, axis, mask):
    count = lax.axis_size(axis)
    return lax.ppermute(block, axis, [(i, i ^ mask) for i in range(count)])


def after(value, earlier):
    return lax.optimization_barrier((value, earlier))[0]


def cut(array, at, size, axis):
    return lax.dynamic_slice_in_dim(array, at * size, size, axis=axis)


def slot_table(seg_replica):
    replica_of = seg_replica[:, 0]
    order = jnp.arange(replica_of.shape[0], dtype=jnp.int32)
    earlier = (replica_of[None, :] == replica_of[:, None]) & (order[None, :] < order[:, None])
    return replica_of, jnp.sum(earlier.astype(jnp.int32), axis=1)


def owner_rows(doc_of_segment, doc_owner):
    owner_of = doc_owner[:, 0]
    doc_ids = jnp.arange(owner_of.shape[0], dtype=jnp.int32)
    earlier = (owner_of[None, :] == owner_of[:, None]) & (doc_ids[None, :] < doc_ids[:, None])
    doc_rank = jnp.sum(earlier.astype(jnp.int32), axis=1)
    start_of = jnp.sum((doc_of_segment[None, :] < doc_ids[:, None]).astype(jnp.int32), axis=1)
    matches = doc_of_segment[:, None] == doc_ids[None, :]
    seg_owner = jnp.sum(jnp.where(matches, owner_of[None, :], 0), axis=1)
    seg_rank = jnp.sum(jnp.where(matches, doc_rank[None, :], 0), axis=1)
    seg_start = jnp.sum(jnp.where(matches, start_of[None, :], 0), axis=1)
    position = jnp.arange(doc_of_segment.shape[0], dtype=jnp.int32) - seg_start
    return seg_owner * (OWN_DOCS * DOC_MOST) + seg_rank * DOC_MOST + position


def room(*arrays):
    total = sum(math.prod(a.shape) * jnp.dtype(a.dtype).itemsize for a in arrays)
    return pltpu.CompilerParams(vmem_limit_bytes=total * 5 // 4 + 6 * 2**20)


def lane_step(width):
    step = 512
    while width % step:
        step //= 2
    return step


def parities():
    rep = lax.axis_index("rep")
    return lax.rem(rep, 2), lax.rem(rep // 2, 2)


def token_kernel(order_ref, x_ref, gain_ref, own_ref, scale_ref, sum_ref):
    slots, count, width = x_ref.shape
    step = lane_step(width)
    for s in range(slots):
        squares = jnp.zeros((count, 128), F32)
        for at in range(0, width, step):
            x = x_ref[s, :, at:at + step].astype(F32)
            sum_ref[s:s + 1, at:at + step] = jnp.sum(x, axis=0, keepdims=True)
            x = x * x
            for i in range(0, step, 128):
                squares += x[:, i:i + 128]
        mean = jnp.sum(squares, axis=1, keepdims=True) * (1.0 / width)
        scale_ref[s * count:(s + 1) * count, :] = jnp.broadcast_to(
            lax.rsqrt(mean + 1e-06), (count, scale_ref.shape[1])
        )


def keyvalue_kernel(length, near_ref, far_ref, gain_ref, own_ref, near_scale_ref, near_sum_ref, query_ref, *refs):
    half_refs, (kv_ref, q_ref, near_out, far_out, scale_ref, mean_ref) = refs[:-6], refs[-6:]
    slots, count, width = near_ref.shape
    rows = slots * count
    step = lane_step(width)
    parts = [own_ref[0], own_ref[1]]
    for here, there in zip(half_refs[::2], half_refs[1::2]):
        parts += [here[0], there[0], here[1], there[1]]
    lanes = kv_ref.shape[1]
    weights = jnp.concatenate(parts + [query_ref[...]], axis=0)
    scale_ref[:rows, :] = near_scale_ref[...]
    for c, (x_ref, out_ref) in enumerate(((near_ref, near_out), (far_ref, far_out))):
        for s in range(slots):
            squares = jnp.zeros((count, 128), F32)
            for at in range(0, width, step):
                x = x_ref[s, :, at:at + step].astype(F32)
                out_ref[s, :, at:at + step] = (x * gain_ref[at:at + step].reshape(1, step)).astype(BF16)
                if c:
                    total = jnp.sum(x, axis=0, keepdims=True) + near_sum_ref[s:s + 1, at:at + step]
                    mean_ref[s:s + 1, at:at + step] = total * (1.0 / length)
                    x = x * x
                    for i in range(0, step, 128):
                        squares += x[:, i:i + 128]
            if c:
                mean = jnp.sum(squares, axis=1, keepdims=True) * (1.0 / width)
                at_row = c * rows + s * count
                scale_ref[at_row:at_row + count, :] = jnp.broadcast_to(
                    lax.rsqrt(mean + 1e-06), (count, scale_ref.shape[1])
                )
        both = lax.dot_general(out_ref[...].reshape(rows, width), weights, NT, preferred_element_type=F32)
        span = slice(c * rows, (c + 1) * rows)
        kv_ref[span, :] = (both[:, :lanes] * scale_ref[span, :1]).astype(BF16)
        q_ref[span, :] = (both[:, lanes:] * scale_ref[span, :]).astype(BF16)


def half_query(x_ref, b_ref, c_ref, turn):
    slots, count, width = x_ref.shape
    part = b_ref.shape[0]
    x_bit, z_bit = parities()
    at_b = pl.multiple_of((x_bit ^ turn) * part, 128)
    at_c = pl.multiple_of((2 + (z_bit ^ turn)) * part, 128)
    rows = slots * count
    total = jnp.dot(
        x_ref[:, :, pl.ds(at_b, part)].reshape(rows, part), b_ref[...], preferred_element_type=F32
    )
    return total + jnp.dot(
        x_ref[:, :, pl.ds(at_c, part)].reshape(rows, part), c_ref[...], preferred_element_type=F32
    )


def query_kernel(order_ref, near_ref, far_ref, *refs):
    n = len(refs) // 3
    part_refs, half_refs = refs[:2 * n], refs[2 * n:]
    slots, count, _ = near_ref.shape
    rows = slots * count
    for c, x_ref in enumerate((near_ref, far_ref)):
        for p, half_ref in enumerate(half_refs):
            half_ref[c * rows:(c + 1) * rows, :] = half_query(x_ref, part_refs[2 * p], part_refs[2 * p + 1], 0)


def product_kernel(masks, order_ref, output_ref, *refs):
    n = len(masks)
    proj_refs, mean_refs, (out_ref, *packed_refs) = refs[:n], refs[n:n * 3 // 2 - 1], refs[n * 3 // 2 - 1:]
    total = jnp.zeros(out_ref.shape, F32)
    for mask, proj_ref in zip(masks, proj_refs):
        total += jnp.dot(output_ref[mask], proj_ref[...], preferred_element_type=F32)
    out_ref[...] = total.astype(BF16)
    height, lanes = out_ref.shape
    for mean_ref, packed_ref in zip(mean_refs, packed_refs):
        packed_ref[:height, :] = total.astype(BF16)
        both = split(mean_ref[...])
        rows, block = both.shape
        for i in range(0, block, lanes):
            take = min(lanes, block - i)
            at = height + i // lanes * rows
            if take < lanes:
                packed_ref[at:at + rows, :] = jnp.zeros((rows, lanes), BF16)
            packed_ref[at:at + rows, :take] = both[:, i:i + take]


def split(value):
    high = value.astype(BF16)
    return jnp.concatenate([high, (value - high.astype(F32)).astype(BF16)], axis=0)


def joined(value):
    half = value.shape[0] // 2
    return value[:half] + value[half:]


def attention_kernel(masks, group, length, *refs):
    n = len(masks)
    at = iter(range(len(refs)))

    def take(count):
        return [refs[next(at)] for _ in range(count)]

    x_refs = take(2)
    scale_ref, query_ref = take(2)
    early_refs, b_refs, c_refs = take(n - 1), take(n - 1), take(n - 1)
    near_refs, far_refs = take(n), take(n)
    w2_refs = [take(2) for _ in range(n)]
    mean_ref, = take(1)
    place_ref, proj_ref, out_ref, q_ref, kv_ref, score_ref, weight_ref, ctx_ref, w2_ref = take(9)
    slots, tokens, _ = x_refs[0].shape
    head_dim = query_ref.shape[1]
    rows = slots * tokens
    groups = sorted({m // group for m in masks})
    heads_of = [[p for p in range(n) if masks[p] // group == g] for g in groups]
    in_group = len(heads_of[0])

    x_bit, _ = parities()
    part = w2_ref.shape[2] // 2
    for p in range(n):
        for i in range(2):
            at_lane = pl.multiple_of((x_bit ^ i) * part, 128)
            w2_ref[p, :, pl.ds(at_lane, part)] = w2_refs[p][i][:head_dim, :]

    for p in range(n):
        for c in range(2):
            mixed = jnp.concatenate(
                [
                    near_refs[p][c * rows:(c + 1) * rows, :],
                    far_refs[p][(1 - c) * rows:(2 - c) * rows, :],
                ],
                axis=1,
            )
            kv_ref[p, c * rows:(c + 1) * rows, :] = jnp.dot(
                mixed, place_ref[p], preferred_element_type=F32
            ).astype(BF16)
    q_ref[0] = query_ref[...]
    for p in range(1, n):
        for c in range(2):
            span = slice(c * rows, (c + 1) * rows)
            q = early_refs[p - 1][span, :] + half_query(x_refs[c], b_refs[p - 1], c_refs[p - 1], 1)
            q_ref[p, span, :] = (q * scale_ref[span, :]).astype(BF16)

    def spans(s):
        return [slice(c * rows + s * tokens, c * rows + (s + 1) * tokens) for c in range(2)]

    def columns(s, first):
        return jnp.concatenate(
            [kv_ref[p, span, first:first + head_dim] for p in range(n) for span in spans(s)], axis=0
        )

    for s in range(slots):
        for g, heads in enumerate(heads_of):
            q = jnp.concatenate([q_ref[p, span, :] for p in heads for span in spans(s)], axis=0)
            keys = columns(s, g * 2 * head_dim)
            score_ref[s, g] = lax.dot_general(q, keys, NT, preferred_element_type=F32)
    for s in range(slots):
        for g in range(len(groups)):
            scores = score_ref[s, g]
            top = jnp.max(scores, axis=1, keepdims=True)
            e = jnp.exp((scores - top) * head_dim ** (-0.5))
            probs = e * (1.0 / jnp.sum(e, axis=1, keepdims=True))
            weight_ref[s, g] = jnp.sum(probs.reshape(in_group, 2 * tokens, -1), axis=1)
    for s in range(slots):
        for g, heads in enumerate(heads_of):
            values = columns(s, (g * 2 + 1) * head_dim)
            context = joined(
                jnp.dot(split(weight_ref[s, g]), values, preferred_element_type=F32)
            ) * (1.0 / length)
            for j, p in enumerate(heads):
                ctx_ref[p, s:s + 1, :] = context[j:j + 1]
    mean = mean_ref[...]
    for p in range(1, n):
        packed = w2_refs[p][0]
        chunks = [
            packed[at:at + 2 * slots, :] for at in range(head_dim, packed.shape[0], 2 * slots)
        ]
        both = jnp.concatenate(chunks, axis=1)[:, :mean.shape[1]]
        mean += joined(both.astype(F32))
    total = joined(jnp.dot(split(mean), proj_ref[...], preferred_element_type=F32))
    for p in range(n):
        total += joined(jnp.dot(split(ctx_ref[p]), w2_ref[p], preferred_element_type=F32))
    out_ref[...] = total


def document_kernel(near_ref, far_ref, select_ref, allow_ref, fill_ref, gain_ref, qkv_ref, out_ref):
    docs, most, head = out_ref.shape
    rows = jnp.concatenate([near_ref[...], far_ref[...]], axis=0)
    high = rows.astype(BF16)
    rest = rows - high.astype(F32)
    middle = rest.astype(BF16)
    low = (rest - middle.astype(F32)).astype(BF16)
    select = select_ref[...].astype(BF16)
    first = sum(jnp.dot(select, part, preferred_element_type=F32) for part in (high, middle, low))
    scale = lax.rsqrt(jnp.mean(first * first, axis=-1, keepdims=True) + 1e-06)
    normed = (first * scale * gain_ref[...]).astype(BF16)
    q, k, v = (
        lax.dot_general(normed, qkv_ref[i], NT, preferred_element_type=F32).astype(BF16) for i in range(3)
    )
    scores = lax.dot_general(q, k, NT, preferred_element_type=F32) * head ** (-0.5)
    scores = jnp.where(allow_ref[...] > 0.5, scores, -1e30)
    e = jnp.exp(scores - jnp.max(scores, axis=1, keepdims=True))
    probs = (e / jnp.sum(e, axis=1, keepdims=True)).astype(BF16)
    context = jnp.dot(probs, v, preferred_element_type=F32) * fill_ref[...]
    for d in range(docs):
        out_ref[d] = context[d * most:(d + 1) * most].astype(BF16)


def local(
    tokens,
    seg_replica,
    doc_of_segment,
    doc_owner,
    enc_gain,
    enc_query,
    enc_keyvalue,
    enc_output,
    doc_proj,
    doc_gain,
    doc_qkv,
):
    n_rep, n_tp = lax.axis_size("rep"), lax.axis_size("tp")
    rep_index = lax.axis_index("rep")
    tp_index = lax.axis_index("tp")
    x_bit, z_bit = rep_index % 2, rep_index // 2 % 2
    slots, own_tokens, width = tokens.shape
    length = own_tokens * n_tp
    head_dim = enc_query.shape[1]
    kv_width = enc_keyvalue.shape[2]
    group = head_dim // kv_width
    block, doc_width = doc_proj.shape
    masks = list(range(0, n_tp, 2))

    kv_rows = jnp.transpose(enc_keyvalue, (1, 2, 0))
    kv_half = cut(kv_rows, x_bit, kv_width // 2, 1)
    kv_y = [flipped(kv_half, "tp", m) for m in masks[1:]]
    tokens_far = flipped(tokens, "tp", 1)
    part_q, part_doc = width // 4, doc_width // 2
    proj = cut(after(doc_proj, kv_half), x_bit, part_doc, 1)
    proj_near = [proj] + [flipped(proj, "tp", m) for m in masks[1:]]
    query_here = after(enc_query, proj)
    b_part, c_part = cut(query_here, x_bit, part_q, 0), cut(query_here, 2 + z_bit, part_q, 0)
    b_y = [flipped(b_part, "tp", m) for m in masks[1:]]
    c_y = [flipped(c_part, "tp", m) for m in masks[1:]]

    query_turned = after(enc_query, (b_part, c_part)).T
    weights = []
    for w in kv_y:
        weights += [w, flipped(w, "rep", 1)]

    rows = slots * own_tokens
    lanes = 2 * kv_width * len(masks)
    out = [
        jax.ShapeDtypeStruct((rows, head_dim), F32),
        jax.ShapeDtypeStruct((slots, width), F32),
    ]
    scale, sums = pl.pallas_call(
        token_kernel,
        in_specs=[pl.BlockSpec(memory_space=pl.ANY)] + [pl.BlockSpec(memory_space=pltpu.VMEM)] * 3,
        out_shape=out,
        compiler_params=room(tokens, enc_gain, kv_rows, *out),
    )(kv_y[0], tokens, enc_gain, kv_rows)
    operands = (tokens, tokens_far, enc_gain, kv_rows, scale, sums, query_turned, *weights)
    out = [
        jax.ShapeDtypeStruct((2 * rows, lanes), BF16),
        jax.ShapeDtypeStruct((2 * rows, head_dim), BF16),
        jax.ShapeDtypeStruct(tokens.shape, BF16),
        jax.ShapeDtypeStruct(tokens.shape, BF16),
        jax.ShapeDtypeStruct((2 * rows, head_dim), F32),
        jax.ShapeDtypeStruct((slots, width), F32),
    ]
    kv, own, near, far, scale, mean = pl.pallas_call(
        functools.partial(keyvalue_kernel, length),
        out_shape=out,
        compiler_params=room(*operands, *out),
    )(*operands)
    kv_near = [kv] + [flipped(kv, "tp", m) for m in masks[1:]]

    proj_near = [after(p, weights[-1]) for p in proj_near]
    proj_all = proj_near + [flipped(p, "tp", 1) for p in proj_near]
    origin = masks + [m + 1 for m in masks]
    output_blocks = jnp.stack([cut(after(enc_output, weights[-1]), tp_index ^ m, block, 1) for m in range(n_tp)], axis=0)
    mean = mean.reshape(slots, n_tp, block)
    means = [lax.dynamic_index_in_dim(mean, tp_index ^ m, 1, keepdims=False) for m in masks]
    height = head_dim + -(-block // part_doc) * 2 * slots
    out = [jax.ShapeDtypeStruct((head_dim, part_doc), BF16)]
    out += [jax.ShapeDtypeStruct((height, part_doc), BF16) for _ in masks[1:]]
    w2, *packed = pl.pallas_call(
        functools.partial(product_kernel, origin),
        in_specs=[pl.BlockSpec(memory_space=pl.ANY)]
        + [pl.BlockSpec(memory_space=pltpu.VMEM)] * (n_tp + len(masks)),
        out_shape=out,
        compiler_params=room(output_blocks, *proj_all, *means, *out),
    )(kv, output_blocks, *proj_all, *means[1:])
    w2_all = [w2, flipped(w2, "rep", 1)]
    for m, p in zip(masks[1:], packed):
        w2_all += [flipped(p, "tp", m), flipped(w2_all[1], "tp", m)]

    count = 2 * lanes
    column = jnp.arange(count, dtype=jnp.int32)
    core = column // lanes
    mask_of = column % lanes // (2 * kv_width) * 2
    inner = column % (2 * kv_width)
    part_kv = kv_width // 2
    quarter = inner // part_kv
    swapped = quarter // 2 * 2 + (quarter % 2 ^ x_bit)
    inner = jnp.where(mask_of == 0, inner, swapped * part_kv + inner % part_kv)
    places = []
    for m in masks:
        target = (
            (mask_of ^ m) // group * (2 * head_dim)
            + inner // kv_width * head_dim
            + (tp_index ^ m ^ mask_of ^ core) % group * kv_width
            + inner % kv_width
        )
        places.append((target[:, None] == column[None, :]).astype(BF16))
    place = jnp.stack(places, axis=0)

    parts, b_rest, c_rest = [], [], []
    for q_b, q_c in zip(b_y, c_y):
        q_b, q_c = after((q_b, q_c), kv)
        parts += [q_b, q_c]
        b_rest.append(flipped(q_b, "rep", 1))
        c_rest.append(flipped(q_c, "rep", 2))
    operands = (near, far, *parts)
    out = [jax.ShapeDtypeStruct((2 * rows, head_dim), F32) for _ in masks[1:]]
    early = pl.pallas_call(
        query_kernel,
        in_specs=[pl.BlockSpec(memory_space=pl.ANY)]
        + [pl.BlockSpec(memory_space=pltpu.VMEM)] * len(operands),
        out_shape=out,
        compiler_params=room(*operands, *out),
    )(w2_all[1], *operands)

    kv_far = [flipped(after(k, (kv_near[1:], early, w2_all[-1])), "tp", 1) for k in kv_near]
    n = len(masks)
    groups = n_tp // group
    operands = (
        near,
        far,
        scale,
        own,
        *early,
        *b_rest,
        *c_rest,
        *kv_near,
        *kv_far,
        *w2_all,
        means[0],
        place,
        doc_proj,
    )
    scratch = [
        pltpu.VMEM((n, 2 * rows, head_dim), BF16),
        pltpu.VMEM((n, 2 * rows, 2 * lanes), BF16),
        pltpu.VMEM((slots, groups, n // groups * 2 * own_tokens, length), F32),
        pltpu.VMEM((slots, groups, n // groups, length), F32),
        pltpu.VMEM((n, slots, head_dim), F32),
        pltpu.VMEM((n, head_dim, doc_width), BF16),
    ]
    part = pl.pallas_call(
        functools.partial(attention_kernel, masks, group, length),
        out_shape=jax.ShapeDtypeStruct((slots, doc_width), F32),
        scratch_shapes=scratch,
        compiler_params=room(*operands, *scratch),
    )(*operands)

    part = part + flipped(part, "tp", 1) + flipped(part, "tp", 2) + flipped(part, "tp", 3)
    bit = 4
    while bit < n_tp:
        part = part + flipped(part, "tp", bit)
        bit *= 2
    bit = 1
    while bit < n_rep // 2:
        part = jnp.concatenate([part, flipped(part, "rep", bit)], axis=0)
        bit *= 2
    part_far = flipped(part, "rep", bit)

    seg_replica, doc_of_segment, doc_owner = after((seg_replica, doc_of_segment, doc_owner), kv)
    replica_of, rank = slot_table(seg_replica)
    row_of = owner_rows(doc_of_segment, doc_owner)
    owned = OWN_DOCS * DOC_MOST
    wanted = rep_index * owned + jnp.arange(owned, dtype=jnp.int32)
    matches = (row_of[None, :] == wanted[:, None]).astype(F32)
    at_slot = (replica_of ^ rep_index) * CAP + rank
    holds = (at_slot[:, None] == jnp.arange(n_rep * CAP, dtype=jnp.int32)[None, :]).astype(F32)
    select = jnp.dot(matches, holds)
    filled = jnp.sum(matches, axis=1)
    row = jnp.arange(owned, dtype=jnp.int32)
    same_doc = row[:, None] // DOC_MOST == row[None, :] // DOC_MOST
    allowed = same_doc & ((filled[None, :] > 0.5) | (row[:, None] == row[None, :]))

    operands = (
        part,
        part_far,
        select,
        allowed.astype(F32),
        filled[:, None],
        doc_gain[None, :],
        jnp.transpose(doc_qkv, (1, 2, 0)),
    )
    return pl.pallas_call(
        document_kernel,
        out_shape=jax.ShapeDtypeStruct((OWN_DOCS, DOC_MOST, doc_qkv.shape[2]), BF16),
        compiler_params=room(*operands),
    )(*operands)


def solution(mesh):
    in_specs = (
        P("rep", "tp", None),
        P(),
        P(),
        P(),
        P(),
        P(None, "tp"),
        P(None, None, "tp"),
        P("tp", None),
        P("tp", None),
        P(),
        P(None, None, "tp"),
    )
    out_specs = P("rep", None, "tp")
    return jax.shard_map(local, mesh=mesh, in_specs=in_specs, out_specs=out_specs, check_vma=False)
```

```python
import functools
import math

import jax
import jax.numpy as jnp
from jax import lax
from jax.experimental import pallas as pl
from jax.experimental.pallas import tpu as pltpu
from jax.sharding import PartitionSpec as P

CAP = 8
DOC_MOST = 4
OWN_DOCS = 4
F32 = jnp.float32
BF16 = jnp.bfloat16
NT = (((1,), (1,)), ((), ()))


def flipped(block, axis, mask):
    count = lax.axis_size(axis)
    return lax.ppermute(block, axis, [(i, i ^ mask) for i in range(count)])


def after(value, earlier):
    return lax.optimization_barrier((value, earlier))[0]


def cut(array, at, size, axis):
    return lax.dynamic_slice_in_dim(array, at * size, size, axis=axis)


def slot_table(seg_replica):
    replica_of = seg_replica[:, 0]
    order = jnp.arange(replica_of.shape[0], dtype=jnp.int32)
    earlier = (replica_of[None, :] == replica_of[:, None]) & (order[None, :] < order[:, None])
    return replica_of, jnp.sum(earlier.astype(jnp.int32), axis=1)


def owner_rows(doc_of_segment, doc_owner):
    owner_of = doc_owner[:, 0]
    doc_ids = jnp.arange(owner_of.shape[0], dtype=jnp.int32)
    earlier = (owner_of[None, :] == owner_of[:, None]) & (doc_ids[None, :] < doc_ids[:, None])
    doc_rank = jnp.sum(earlier.astype(jnp.int32), axis=1)
    start_of = jnp.sum((doc_of_segment[None, :] < doc_ids[:, None]).astype(jnp.int32), axis=1)
    matches = doc_of_segment[:, None] == doc_ids[None, :]
    seg_owner = jnp.sum(jnp.where(matches, owner_of[None, :], 0), axis=1)
    seg_rank = jnp.sum(jnp.where(matches, doc_rank[None, :], 0), axis=1)
    seg_start = jnp.sum(jnp.where(matches, start_of[None, :], 0), axis=1)
    position = jnp.arange(doc_of_segment.shape[0], dtype=jnp.int32) - seg_start
    return seg_owner * (OWN_DOCS * DOC_MOST) + seg_rank * DOC_MOST + position


def room(*arrays):
    total = sum(math.prod(a.shape) * jnp.dtype(a.dtype).itemsize for a in arrays)
    return pltpu.CompilerParams(vmem_limit_bytes=total * 5 // 4 + 6 * 2**20)


def lane_step(width):
    step = 512
    while width % step:
        step //= 2
    return step


def parities():
    rep = lax.axis_index("rep")
    return lax.rem(rep, 2), lax.rem(rep // 2, 2)


def token_kernel(order_ref, x_ref, gain_ref, own_ref, scale_ref, sum_ref):
    slots, count, width = x_ref.shape
    step = lane_step(width)
    for s in range(slots):
        squares = jnp.zeros((count, 128), F32)
        for at in range(0, width, step):
            x = x_ref[s, :, at:at + step].astype(F32)
            sum_ref[s:s + 1, at:at + step] = jnp.sum(x, axis=0, keepdims=True)
            x = x * x
            for i in range(0, step, 128):
                squares += x[:, i:i + 128]
        mean = jnp.sum(squares, axis=1, keepdims=True) * (1.0 / width)
        scale_ref[s * count:(s + 1) * count, :] = jnp.broadcast_to(
            lax.rsqrt(mean + 1e-06), (count, scale_ref.shape[1])
        )


def keyvalue_kernel(length, near_ref, far_ref, gain_ref, own_ref, near_scale_ref, near_sum_ref, query_ref, *refs):
    half_refs, (kv_ref, q_ref, near_out, far_out, scale_ref, mean_ref) = refs[:-6], refs[-6:]
    slots, count, width = near_ref.shape
    rows = slots * count
    step = lane_step(width)
    parts = [own_ref[0], own_ref[1]]
    for here, there in zip(half_refs[::2], half_refs[1::2]):
        parts += [here[0], there[0], here[1], there[1]]
    lanes = kv_ref.shape[1]
    weights = jnp.concatenate(parts + [query_ref[...]], axis=0)
    scale_ref[:rows, :] = near_scale_ref[...]
    for c, (x_ref, out_ref) in enumerate(((near_ref, near_out), (far_ref, far_out))):
        for s in range(slots):
            squares = jnp.zeros((count, 128), F32)
            for at in range(0, width, step):
                x = x_ref[s, :, at:at + step].astype(F32)
                out_ref[s, :, at:at + step] = (x * gain_ref[at:at + step].reshape(1, step)).astype(BF16)
                if c:
                    total = jnp.sum(x, axis=0, keepdims=True) + near_sum_ref[s:s + 1, at:at + step]
                    mean_ref[s:s + 1, at:at + step] = total * (1.0 / length)
                    x = x * x
                    for i in range(0, step, 128):
                        squares += x[:, i:i + 128]
            if c:
                mean = jnp.sum(squares, axis=1, keepdims=True) * (1.0 / width)
                at_row = c * rows + s * count
                scale_ref[at_row:at_row + count, :] = jnp.broadcast_to(
                    lax.rsqrt(mean + 1e-06), (count, scale_ref.shape[1])
                )
        both = lax.dot_general(out_ref[...].reshape(rows, width), weights, NT, preferred_element_type=F32)
        span = slice(c * rows, (c + 1) * rows)
        kv_ref[span, :] = (both[:, :lanes] * scale_ref[span, :1]).astype(BF16)
        q_ref[span, :] = (both[:, lanes:] * scale_ref[span, :]).astype(BF16)


def half_query(x_ref, b_ref, c_ref, turn):
    slots, count, width = x_ref.shape
    part = b_ref.shape[0]
    x_bit, z_bit = parities()
    at_b = pl.multiple_of((x_bit ^ turn) * part, 128)
    at_c = pl.multiple_of((2 + (z_bit ^ turn)) * part, 128)
    rows = slots * count
    total = jnp.dot(
        x_ref[:, :, pl.ds(at_b, part)].reshape(rows, part), b_ref[...], preferred_element_type=F32
    )
    return total + jnp.dot(
        x_ref[:, :, pl.ds(at_c, part)].reshape(rows, part), c_ref[...], preferred_element_type=F32
    )


def query_kernel(order_ref, near_ref, far_ref, *refs):
    n = len(refs) // 3
    part_refs, half_refs = refs[:2 * n], refs[2 * n:]
    slots, count, _ = near_ref.shape
    rows = slots * count
    for c, x_ref in enumerate((near_ref, far_ref)):
        for p, half_ref in enumerate(half_refs):
            half_ref[c * rows:(c + 1) * rows, :] = half_query(x_ref, part_refs[2 * p], part_refs[2 * p + 1], 0)


def product_kernel(masks, order_ref, output_ref, *refs):
    n = len(masks)
    proj_refs, mean_refs, (out_ref, *packed_refs) = refs[:n], refs[n:n * 3 // 2 - 1], refs[n * 3 // 2 - 1:]
    total = jnp.zeros(out_ref.shape, F32)
    for mask, proj_ref in zip(masks, proj_refs):
        total += jnp.dot(output_ref[mask], proj_ref[...], preferred_element_type=F32)
    out_ref[...] = total.astype(BF16)
    height, lanes = out_ref.shape
    for mean_ref, packed_ref in zip(mean_refs, packed_refs):
        packed_ref[:height, :] = total.astype(BF16)
        both = split(mean_ref[...])
        rows, block = both.shape
        for i in range(0, block, lanes):
            take = min(lanes, block - i)
            at = height + i // lanes * rows
            if take < lanes:
                packed_ref[at:at + rows, :] = jnp.zeros((rows, lanes), BF16)
            packed_ref[at:at + rows, :take] = both[:, i:i + take]


def split(value):
    high = value.astype(BF16)
    return jnp.concatenate([high, (value - high.astype(F32)).astype(BF16)], axis=0)


def joined(value):
    half = value.shape[0] // 2
    return value[:half] + value[half:]


def attention_kernel(masks, group, length, *refs):
    n = len(masks)
    at = iter(range(len(refs)))

    def take(count):
        return [refs[next(at)] for _ in range(count)]

    x_refs = take(2)
    scale_ref, query_ref = take(2)
    early_refs, b_refs, c_refs = take(n - 1), take(n - 1), take(n - 1)
    near_refs, far_refs = take(n), take(n)
    w2_refs = [take(2) for _ in range(n)]
    mean_ref, = take(1)
    place_ref, proj_ref, out_ref, q_ref, kv_ref, score_ref, weight_ref, ctx_ref, w2_ref = take(9)
    slots, tokens, _ = x_refs[0].shape
    head_dim = query_ref.shape[1]
    rows = slots * tokens
    groups = sorted({m // group for m in masks})
    heads_of = [[p for p in range(n) if masks[p] // group == g] for g in groups]
    in_group = len(heads_of[0])

    x_bit, _ = parities()
    part = w2_ref.shape[2] // 2
    for p in range(n):
        for i in range(2):
            at_lane = pl.multiple_of((x_bit ^ i) * part, 128)
            w2_ref[p, :, pl.ds(at_lane, part)] = w2_refs[p][i][:head_dim, :]

    for p in range(n):
        for c in range(2):
            mixed = jnp.concatenate(
                [
                    near_refs[p][c * rows:(c + 1) * rows, :],
                    far_refs[p][(1 - c) * rows:(2 - c) * rows, :],
                ],
                axis=1,
            )
            kv_ref[p, c * rows:(c + 1) * rows, :] = jnp.dot(
                mixed, place_ref[p], preferred_element_type=F32
            ).astype(BF16)
    q_ref[0] = query_ref[...]
    for p in range(1, n):
        for c in range(2):
            span = slice(c * rows, (c + 1) * rows)
            q = early_refs[p - 1][span, :] + half_query(x_refs[c], b_refs[p - 1], c_refs[p - 1], 1)
            q_ref[p, span, :] = (q * scale_ref[span, :]).astype(BF16)

    def spans(s):
        return [slice(c * rows + s * tokens, c * rows + (s + 1) * tokens) for c in range(2)]

    def columns(s, first):
        return jnp.concatenate(
            [kv_ref[p, span, first:first + head_dim] for p in range(n) for span in spans(s)], axis=0
        )

    for s in range(slots):
        for g, heads in enumerate(heads_of):
            q = jnp.concatenate([q_ref[p, span, :] for p in heads for span in spans(s)], axis=0)
            keys = columns(s, g * 2 * head_dim)
            score_ref[s, g] = lax.dot_general(q, keys, NT, preferred_element_type=F32)
    for s in range(slots):
        for g in range(len(groups)):
            scores = score_ref[s, g]
            top = jnp.max(scores, axis=1, keepdims=True)
            e = jnp.exp((scores - top) * head_dim ** (-0.5))
            probs = e * (1.0 / jnp.sum(e, axis=1, keepdims=True))
            weight_ref[s, g] = jnp.sum(probs.reshape(in_group, 2 * tokens, -1), axis=1)
    for s in range(slots):
        for g, heads in enumerate(heads_of):
            values = columns(s, (g * 2 + 1) * head_dim)
            context = joined(
                jnp.dot(split(weight_ref[s, g]), values, preferred_element_type=F32)
            ) * (1.0 / length)
            for j, p in enumerate(heads):
                ctx_ref[p, s:s + 1, :] = context[j:j + 1]
    mean = mean_ref[...]
    for p in range(1, n):
        packed = w2_refs[p][0]
        chunks = [
            packed[at:at + 2 * slots, :] for at in range(head_dim, packed.shape[0], 2 * slots)
        ]
        both = jnp.concatenate(chunks, axis=1)[:, :mean.shape[1]]
        mean += joined(both.astype(F32))
    total = joined(jnp.dot(split(mean), proj_ref[...], preferred_element_type=F32))
    for p in range(n):
        total += joined(jnp.dot(split(ctx_ref[p]), w2_ref[p], preferred_element_type=F32))
    out_ref[...] = total


def document_kernel(near_ref, far_ref, select_ref, allow_ref, fill_ref, gain_ref, qkv_ref, out_ref):
    docs, most, head = out_ref.shape
    rows = jnp.concatenate([near_ref[...], far_ref[...]], axis=0)
    high = rows.astype(BF16)
    rest = rows - high.astype(F32)
    middle = rest.astype(BF16)
    low = (rest - middle.astype(F32)).astype(BF16)
    select = select_ref[...].astype(BF16)
    first = sum(jnp.dot(select, part, preferred_element_type=F32) for part in (high, middle, low))
    scale = lax.rsqrt(jnp.mean(first * first, axis=-1, keepdims=True) + 1e-06)
    normed = (first * scale * gain_ref[...]).astype(BF16)
    q, k, v = (
        lax.dot_general(normed, qkv_ref[i], NT, preferred_element_type=F32).astype(BF16) for i in range(3)
    )
    scores = lax.dot_general(q, k, NT, preferred_element_type=F32) * head ** (-0.5)
    scores = jnp.where(allow_ref[...] > 0.5, scores, -1e30)
    e = jnp.exp(scores - jnp.max(scores, axis=1, keepdims=True))
    probs = (e / jnp.sum(e, axis=1, keepdims=True)).astype(BF16)
    context = jnp.dot(probs, v, preferred_element_type=F32) * fill_ref[...]
    for d in range(docs):
        out_ref[d] = context[d * most:(d + 1) * most].astype(BF16)


def local(
    tokens,
    seg_replica,
    doc_of_segment,
    doc_owner,
    enc_gain,
    enc_query,
    enc_keyvalue,
    enc_output,
    doc_proj,
    doc_gain,
    doc_qkv,
):
    n_rep, n_tp = lax.axis_size("rep"), lax.axis_size("tp")
    rep_index = lax.axis_index("rep")
    tp_index = lax.axis_index("tp")
    x_bit, z_bit = rep_index % 2, rep_index // 2 % 2
    slots, own_tokens, width = tokens.shape
    length = own_tokens * n_tp
    head_dim = enc_query.shape[1]
    kv_width = enc_keyvalue.shape[2]
    group = head_dim // kv_width
    block, doc_width = doc_proj.shape
    masks = list(range(0, n_tp, 2))

    kv_rows = jnp.transpose(enc_keyvalue, (1, 2, 0))
    kv_half = cut(kv_rows, x_bit, kv_width // 2, 1)
    kv_y = [flipped(kv_half, "tp", m) for m in masks[1:]]
    tokens_far = flipped(tokens, "tp", 1)
    part_q, part_doc = width // 4, doc_width // 2
    proj = cut(after(doc_proj, kv_half), x_bit, part_doc, 1)
    proj_near = [proj] + [flipped(proj, "tp", m) for m in masks[1:]]
    query_here = after(enc_query, proj)
    b_part, c_part = cut(query_here, x_bit, part_q, 0), cut(query_here, 2 + z_bit, part_q, 0)
    b_y = [flipped(b_part, "tp", m) for m in masks[1:]]
    c_y = [flipped(c_part, "tp", m) for m in masks[1:]]

    query_turned = after(enc_query, (b_part, c_part, kv_y[0])).T
    weights = []
    for w in kv_y:
        weights += [w, flipped(w, "rep", 1)]

    rows = slots * own_tokens
    lanes = 2 * kv_width * len(masks)
    out = [
        jax.ShapeDtypeStruct((rows, head_dim), F32),
        jax.ShapeDtypeStruct((slots, width), F32),
    ]
    scale, sums = pl.pallas_call(
        token_kernel,
        in_specs=[pl.BlockSpec(memory_space=pl.ANY)] + [pl.BlockSpec(memory_space=pltpu.VMEM)] * 3,
        out_shape=out,
        compiler_params=room(tokens, enc_gain, kv_rows, *out),
    )(query_turned, tokens, enc_gain, kv_rows)
    operands = (tokens, tokens_far, enc_gain, kv_rows, scale, sums, query_turned, *weights)
    out = [
        jax.ShapeDtypeStruct((2 * rows, lanes), BF16),
        jax.ShapeDtypeStruct((2 * rows, head_dim), BF16),
        jax.ShapeDtypeStruct(tokens.shape, BF16),
        jax.ShapeDtypeStruct(tokens.shape, BF16),
        jax.ShapeDtypeStruct((2 * rows, head_dim), F32),
        jax.ShapeDtypeStruct((slots, width), F32),
    ]
    kv, own, near, far, scale, mean = pl.pallas_call(
        functools.partial(keyvalue_kernel, length),
        out_shape=out,
        compiler_params=room(*operands, *out),
    )(*operands)
    kv_near = [kv] + [flipped(kv, "tp", m) for m in masks[1:]]

    proj_near = [after(p, weights[-1]) for p in proj_near]
    proj_all = proj_near + [flipped(p, "tp", 1) for p in proj_near]
    origin = masks + [m + 1 for m in masks]
    output_blocks = jnp.stack([cut(after(enc_output, weights[-1]), tp_index ^ m, block, 1) for m in range(n_tp)], axis=0)
    mean = mean.reshape(slots, n_tp, block)
    means = [lax.dynamic_index_in_dim(mean, tp_index ^ m, 1, keepdims=False) for m in masks]
    height = head_dim + -(-block // part_doc) * 2 * slots
    out = [jax.ShapeDtypeStruct((head_dim, part_doc), BF16)]
    out += [jax.ShapeDtypeStruct((height, part_doc), BF16) for _ in masks[1:]]
    w2, *packed = pl.pallas_call(
        functools.partial(product_kernel, origin),
        in_specs=[pl.BlockSpec(memory_space=pl.ANY)]
        + [pl.BlockSpec(memory_space=pltpu.VMEM)] * (n_tp + len(masks)),
        out_shape=out,
        compiler_params=room(output_blocks, *proj_all, *means, *out),
    )(kv, output_blocks, *proj_all, *means[1:])
    w2_all = [w2, flipped(w2, "rep", 1)]
    for m, p in zip(masks[1:], packed):
        w2_all += [flipped(p, "tp", m), flipped(w2_all[1], "tp", m)]

    count = 2 * lanes
    column = jnp.arange(count, dtype=jnp.int32)
    core = column // lanes
    mask_of = column % lanes // (2 * kv_width) * 2
    inner = column % (2 * kv_width)
    part_kv = kv_width // 2
    quarter = inner // part_kv
    swapped = quarter // 2 * 2 + (quarter % 2 ^ x_bit)
    inner = jnp.where(mask_of == 0, inner, swapped * part_kv + inner % part_kv)
    places = []
    for m in masks:
        target = (
            (mask_of ^ m) // group * (2 * head_dim)
            + inner // kv_width * head_dim
            + (tp_index ^ m ^ mask_of ^ core) % group * kv_width
            + inner % kv_width
        )
        places.append((target[:, None] == column[None, :]).astype(BF16))
    place = jnp.stack(places, axis=0)

    parts, b_rest, c_rest = [], [], []
    for q_b, q_c in zip(b_y, c_y):
        q_b, q_c = after((q_b, q_c), kv)
        parts += [q_b, q_c]
        b_rest.append(flipped(q_b, "rep", 1))
        c_rest.append(flipped(q_c, "rep", 2))
    operands = (near, far, *parts)
    out = [jax.ShapeDtypeStruct((2 * rows, head_dim), F32) for _ in masks[1:]]
    early = pl.pallas_call(
        query_kernel,
        in_specs=[pl.BlockSpec(memory_space=pl.ANY)]
        + [pl.BlockSpec(memory_space=pltpu.VMEM)] * len(operands),
        out_shape=out,
        compiler_params=room(*operands, *out),
    )(w2_all[1], *operands)

    kv_far = [flipped(after(k, (kv_near[1:], early, w2_all[-1])), "tp", 1) for k in kv_near]
    n = len(masks)
    groups = n_tp // group
    operands = (
        near,
        far,
        scale,
        own,
        *early,
        *b_rest,
        *c_rest,
        *kv_near,
        *kv_far,
        *w2_all,
        means[0],
        place,
        doc_proj,
    )
    scratch = [
        pltpu.VMEM((n, 2 * rows, head_dim), BF16),
        pltpu.VMEM((n, 2 * rows, 2 * lanes), BF16),
        pltpu.VMEM((slots, groups, n // groups * 2 * own_tokens, length), F32),
        pltpu.VMEM((slots, groups, n // groups, length), F32),
        pltpu.VMEM((n, slots, head_dim), F32),
        pltpu.VMEM((n, head_dim, doc_width), BF16),
    ]
    part = pl.pallas_call(
        functools.partial(attention_kernel, masks, group, length),
        out_shape=jax.ShapeDtypeStruct((slots, doc_width), F32),
        scratch_shapes=scratch,
        compiler_params=room(*operands, *scratch),
    )(*operands)

    part = part + flipped(part, "tp", 1) + flipped(part, "tp", 2) + flipped(part, "tp", 3)
    bit = 4
    while bit < n_tp:
        part = part + flipped(part, "tp", bit)
        bit *= 2
    bit = 1
    while bit < n_rep // 2:
        part = jnp.concatenate([part, flipped(part, "rep", bit)], axis=0)
        bit *= 2
    part_far = flipped(part, "rep", bit)

    seg_replica, doc_of_segment, doc_owner = after((seg_replica, doc_of_segment, doc_owner), kv)
    replica_of, rank = slot_table(seg_replica)
    row_of = owner_rows(doc_of_segment, doc_owner)
    owned = OWN_DOCS * DOC_MOST
    wanted = rep_index * owned + jnp.arange(owned, dtype=jnp.int32)
    matches = (row_of[None, :] == wanted[:, None]).astype(F32)
    at_slot = (replica_of ^ rep_index) * CAP + rank
    holds = (at_slot[:, None] == jnp.arange(n_rep * CAP, dtype=jnp.int32)[None, :]).astype(F32)
    select = jnp.dot(matches, holds)
    filled = jnp.sum(matches, axis=1)
    row = jnp.arange(owned, dtype=jnp.int32)
    same_doc = row[:, None] // DOC_MOST == row[None, :] // DOC_MOST
    allowed = same_doc & ((filled[None, :] > 0.5) | (row[:, None] == row[None, :]))

    operands = (
        part,
        part_far,
        select,
        allowed.astype(F32),
        filled[:, None],
        doc_gain[None, :],
        jnp.transpose(doc_qkv, (1, 2, 0)),
    )
    return pl.pallas_call(
        document_kernel,
        out_shape=jax.ShapeDtypeStruct((OWN_DOCS, DOC_MOST, doc_qkv.shape[2]), BF16),
        compiler_params=room(*operands),
    )(*operands)


def solution(mesh):
    in_specs = (
        P("rep", "tp", None),
        P(),
        P(),
        P(),
        P(),
        P(None, "tp"),
        P(None, None, "tp"),
        P("tp", None),
        P("tp", None),
        P(),
        P(None, None, "tp"),
    )
    out_specs = P("rep", None, "tp")
    return jax.shard_map(local, mesh=mesh, in_specs=in_specs, out_specs=out_specs, check_vma=False)
```

```python
import functools
import math

import jax
import jax.numpy as jnp
from jax import lax
from jax.experimental import pallas as pl
from jax.experimental.pallas import tpu as pltpu
from jax.sharding import PartitionSpec as P

CAP = 8
DOC_MOST = 4
OWN_DOCS = 4
F32 = jnp.float32
BF16 = jnp.bfloat16
NT = (((1,), (1,)), ((), ()))


def flipped(block, axis, mask):
    count = lax.axis_size(axis)
    return lax.ppermute(block, axis, [(i, i ^ mask) for i in range(count)])


def after(value, earlier):
    return lax.optimization_barrier((value, earlier))[0]


def cut(array, at, size, axis):
    return lax.dynamic_slice_in_dim(array, at * size, size, axis=axis)


def slot_table(seg_replica):
    replica_of = seg_replica[:, 0]
    order = jnp.arange(replica_of.shape[0], dtype=jnp.int32)
    earlier = (replica_of[None, :] == replica_of[:, None]) & (order[None, :] < order[:, None])
    return replica_of, jnp.sum(earlier.astype(jnp.int32), axis=1)


def owner_rows(doc_of_segment, doc_owner):
    owner_of = doc_owner[:, 0]
    doc_ids = jnp.arange(owner_of.shape[0], dtype=jnp.int32)
    earlier = (owner_of[None, :] == owner_of[:, None]) & (doc_ids[None, :] < doc_ids[:, None])
    doc_rank = jnp.sum(earlier.astype(jnp.int32), axis=1)
    start_of = jnp.sum((doc_of_segment[None, :] < doc_ids[:, None]).astype(jnp.int32), axis=1)
    matches = doc_of_segment[:, None] == doc_ids[None, :]
    seg_owner = jnp.sum(jnp.where(matches, owner_of[None, :], 0), axis=1)
    seg_rank = jnp.sum(jnp.where(matches, doc_rank[None, :], 0), axis=1)
    seg_start = jnp.sum(jnp.where(matches, start_of[None, :], 0), axis=1)
    position = jnp.arange(doc_of_segment.shape[0], dtype=jnp.int32) - seg_start
    return seg_owner * (OWN_DOCS * DOC_MOST) + seg_rank * DOC_MOST + position


def room(*arrays):
    total = sum(math.prod(a.shape) * jnp.dtype(a.dtype).itemsize for a in arrays)
    return pltpu.CompilerParams(vmem_limit_bytes=total * 5 // 4 + 6 * 2**20)


def lane_step(width):
    step = 512
    while width % step:
        step //= 2
    return step


def parities():
    rep = lax.axis_index("rep")
    return lax.rem(rep, 2), lax.rem(rep // 2, 2)


def token_kernel(order_ref, x_ref, gain_ref, own_ref, scale_ref, sum_ref):
    slots, count, width = x_ref.shape
    step = lane_step(width)
    for s in range(slots):
        squares = jnp.zeros((count, 128), F32)
        for at in range(0, width, step):
            x = x_ref[s, :, at:at + step].astype(F32)
            sum_ref[s:s + 1, at:at + step] = jnp.sum(x, axis=0, keepdims=True)
            x = x * x
            for i in range(0, step, 128):
                squares += x[:, i:i + 128]
        mean = jnp.sum(squares, axis=1, keepdims=True) * (1.0 / width)
        scale_ref[s * count:(s + 1) * count, :] = jnp.broadcast_to(
            lax.rsqrt(mean + 1e-06), (count, scale_ref.shape[1])
        )


def keyvalue_kernel(length, near_ref, far_ref, gain_ref, own_ref, near_scale_ref, near_sum_ref, query_ref, *refs):
    half_refs, (kv_ref, q_ref, near_out, far_out, scale_ref, mean_ref) = refs[:-6], refs[-6:]
    slots, count, width = near_ref.shape
    rows = slots * count
    step = lane_step(width)
    parts = [own_ref[0], own_ref[1]]
    for here, there in zip(half_refs[::2], half_refs[1::2]):
        parts += [here[0], there[0], here[1], there[1]]
    lanes = kv_ref.shape[1]
    weights = jnp.concatenate(parts + [query_ref[...]], axis=0)
    scale_ref[:rows, :] = near_scale_ref[...]
    for c, (x_ref, out_ref) in enumerate(((near_ref, near_out), (far_ref, far_out))):
        for s in range(slots):
            squares = jnp.zeros((count, 128), F32)
            for at in range(0, width, step):
                x = x_ref[s, :, at:at + step].astype(F32)
                out_ref[s, :, at:at + step] = (x * gain_ref[at:at + step].reshape(1, step)).astype(BF16)
                if c:
                    total = jnp.sum(x, axis=0, keepdims=True) + near_sum_ref[s:s + 1, at:at + step]
                    mean_ref[s:s + 1, at:at + step] = total * (1.0 / length)
                    x = x * x
                    for i in range(0, step, 128):
                        squares += x[:, i:i + 128]
            if c:
                mean = jnp.sum(squares, axis=1, keepdims=True) * (1.0 / width)
                at_row = c * rows + s * count
                scale_ref[at_row:at_row + count, :] = jnp.broadcast_to(
                    lax.rsqrt(mean + 1e-06), (count, scale_ref.shape[1])
                )
        both = lax.dot_general(out_ref[...].reshape(rows, width), weights, NT, preferred_element_type=F32)
        span = slice(c * rows, (c + 1) * rows)
        kv_ref[span, :] = (both[:, :lanes] * scale_ref[span, :1]).astype(BF16)
        q_ref[span, :] = (both[:, lanes:] * scale_ref[span, :]).astype(BF16)


def half_query(x_ref, b_ref, c_ref, turn):
    slots, count, width = x_ref.shape
    part = b_ref.shape[0]
    x_bit, z_bit = parities()
    at_b = pl.multiple_of((x_bit ^ turn) * part, 128)
    at_c = pl.multiple_of((2 + (z_bit ^ turn)) * part, 128)
    rows = slots * count
    total = jnp.dot(
        x_ref[:, :, pl.ds(at_b, part)].reshape(rows, part), b_ref[...], preferred_element_type=F32
    )
    return total + jnp.dot(
        x_ref[:, :, pl.ds(at_c, part)].reshape(rows, part), c_ref[...], preferred_element_type=F32
    )


def query_kernel(order_ref, near_ref, far_ref, *refs):
    n = len(refs) // 3
    part_refs, half_refs = refs[:2 * n], refs[2 * n:]
    slots, count, _ = near_ref.shape
    rows = slots * count
    for c, x_ref in enumerate((near_ref, far_ref)):
        for p, half_ref in enumerate(half_refs):
            half_ref[c * rows:(c + 1) * rows, :] = half_query(x_ref, part_refs[2 * p], part_refs[2 * p + 1], 0)


def product_kernel(masks, order_ref, output_ref, *refs):
    n = len(masks)
    proj_refs, mean_refs, (out_ref, *packed_refs) = refs[:n], refs[n:n * 3 // 2 - 1], refs[n * 3 // 2 - 1:]
    total = jnp.zeros(out_ref.shape, F32)
    for mask, proj_ref in zip(masks, proj_refs):
        total += jnp.dot(output_ref[mask], proj_ref[...], preferred_element_type=F32)
    out_ref[...] = total.astype(BF16)
    height, lanes = out_ref.shape
    for mean_ref, packed_ref in zip(mean_refs, packed_refs):
        packed_ref[:height, :] = total.astype(BF16)
        both = split(mean_ref[...])
        rows, block = both.shape
        for i in range(0, block, lanes):
            take = min(lanes, block - i)
            at = height + i // lanes * rows
            if take < lanes:
                packed_ref[at:at + rows, :] = jnp.zeros((rows, lanes), BF16)
            packed_ref[at:at + rows, :take] = both[:, i:i + take]


def split(value):
    high = value.astype(BF16)
    return jnp.concatenate([high, (value - high.astype(F32)).astype(BF16)], axis=0)


def joined(value):
    half = value.shape[0] // 2
    return value[:half] + value[half:]


def attention_kernel(masks, group, length, *refs):
    n = len(masks)
    at = iter(range(len(refs)))

    def take(count):
        return [refs[next(at)] for _ in range(count)]

    x_refs = take(2)
    scale_ref, query_ref = take(2)
    early_refs, b_refs, c_refs = take(n - 1), take(n - 1), take(n - 1)
    near_refs, far_refs = take(n), take(n)
    w2_refs = [take(2) for _ in range(n)]
    mean_ref, = take(1)
    place_ref, proj_ref, out_ref, q_ref, kv_ref, score_ref, weight_ref, ctx_ref, w2_ref = take(9)
    slots, tokens, _ = x_refs[0].shape
    head_dim = query_ref.shape[1]
    rows = slots * tokens
    groups = sorted({m // group for m in masks})
    heads_of = [[p for p in range(n) if masks[p] // group == g] for g in groups]
    in_group = len(heads_of[0])

    x_bit, _ = parities()
    part = w2_ref.shape[2] // 2
    for p in range(n):
        for i in range(2):
            at_lane = pl.multiple_of((x_bit ^ i) * part, 128)
            w2_ref[p, :, pl.ds(at_lane, part)] = w2_refs[p][i][:head_dim, :]

    for p in range(n):
        for c in range(2):
            mixed = jnp.concatenate(
                [
                    near_refs[p][c * rows:(c + 1) * rows, :],
                    far_refs[p][(1 - c) * rows:(2 - c) * rows, :],
                ],
                axis=1,
            )
            kv_ref[p, c * rows:(c + 1) * rows, :] = jnp.dot(
                mixed, place_ref[p], preferred_element_type=F32
            ).astype(BF16)
    q_ref[0] = query_ref[...]
    for p in range(1, n):
        for c in range(2):
            span = slice(c * rows, (c + 1) * rows)
            q = early_refs[p - 1][span, :] + half_query(x_refs[c], b_refs[p - 1], c_refs[p - 1], 1)
            q_ref[p, span, :] = (q * scale_ref[span, :]).astype(BF16)

    def spans(s):
        return [slice(c * rows + s * tokens, c * rows + (s + 1) * tokens) for c in range(2)]

    def columns(s, first):
        return jnp.concatenate(
            [kv_ref[p, span, first:first + head_dim] for p in range(n) for span in spans(s)], axis=0
        )

    for s in range(slots):
        for g, heads in enumerate(heads_of):
            q = jnp.concatenate([q_ref[p, span, :] for p in heads for span in spans(s)], axis=0)
            keys = columns(s, g * 2 * head_dim)
            score_ref[s, g] = lax.dot_general(q, keys, NT, preferred_element_type=F32)
    for s in range(slots):
        for g in range(len(groups)):
            scores = score_ref[s, g]
            top = jnp.max(scores, axis=1, keepdims=True)
            e = jnp.exp((scores - top) * head_dim ** (-0.5))
            probs = e * (1.0 / jnp.sum(e, axis=1, keepdims=True))
            weight_ref[s, g] = jnp.sum(probs.reshape(in_group, 2 * tokens, -1), axis=1)
    for s in range(slots):
        for g, heads in enumerate(heads_of):
            values = columns(s, (g * 2 + 1) * head_dim)
            context = joined(
                jnp.dot(split(weight_ref[s, g]), values, preferred_element_type=F32)
            ) * (1.0 / length)
            for j, p in enumerate(heads):
                ctx_ref[p, s:s + 1, :] = context[j:j + 1]
    mean = mean_ref[...]
    for p in range(1, n):
        packed = w2_refs[p][0]
        chunks = [
            packed[at:at + 2 * slots, :] for at in range(head_dim, packed.shape[0], 2 * slots)
        ]
        both = jnp.concatenate(chunks, axis=1)[:, :mean.shape[1]]
        mean += joined(both.astype(F32))
    total = joined(jnp.dot(split(mean), proj_ref[...], preferred_element_type=F32))
    for p in range(n):
        total += joined(jnp.dot(split(ctx_ref[p]), w2_ref[p], preferred_element_type=F32))
    out_ref[...] = total


def document_kernel(near_ref, far_ref, select_ref, allow_ref, fill_ref, gain_ref, qkv_ref, out_ref):
    docs, most, head = out_ref.shape
    rows = jnp.concatenate([near_ref[...], far_ref[...]], axis=0)
    high = rows.astype(BF16)
    rest = rows - high.astype(F32)
    middle = rest.astype(BF16)
    low = (rest - middle.astype(F32)).astype(BF16)
    select = select_ref[...].astype(BF16)
    first = sum(jnp.dot(select, part, preferred_element_type=F32) for part in (high, middle, low))
    scale = lax.rsqrt(jnp.mean(first * first, axis=-1, keepdims=True) + 1e-06)
    normed = (first * scale * gain_ref[...]).astype(BF16)
    q, k, v = (
        lax.dot_general(normed, qkv_ref[i], NT, preferred_element_type=F32).astype(BF16) for i in range(3)
    )
    scores = lax.dot_general(q, k, NT, preferred_element_type=F32) * head ** (-0.5)
    scores = jnp.where(allow_ref[...] > 0.5, scores, -1e30)
    e = jnp.exp(scores - jnp.max(scores, axis=1, keepdims=True))
    probs = (e / jnp.sum(e, axis=1, keepdims=True)).astype(BF16)
    context = jnp.dot(probs, v, preferred_element_type=F32) * fill_ref[...]
    for d in range(docs):
        out_ref[d] = context[d * most:(d + 1) * most].astype(BF16)


def local(
    tokens,
    seg_replica,
    doc_of_segment,
    doc_owner,
    enc_gain,
    enc_query,
    enc_keyvalue,
    enc_output,
    doc_proj,
    doc_gain,
    doc_qkv,
):
    n_rep, n_tp = lax.axis_size("rep"), lax.axis_size("tp")
    rep_index = lax.axis_index("rep")
    tp_index = lax.axis_index("tp")
    x_bit, z_bit = rep_index % 2, rep_index // 2 % 2
    slots, own_tokens, width = tokens.shape
    length = own_tokens * n_tp
    head_dim = enc_query.shape[1]
    kv_width = enc_keyvalue.shape[2]
    group = head_dim // kv_width
    block, doc_width = doc_proj.shape
    masks = list(range(0, n_tp, 2))

    kv_rows = jnp.transpose(enc_keyvalue, (1, 2, 0))
    kv_half = cut(kv_rows, x_bit, kv_width // 2, 1)
    kv_y = [flipped(kv_half, "tp", m) for m in masks[1:]]
    tokens_far = flipped(tokens, "tp", 1)
    part_q, part_doc = width // 4, doc_width // 2
    proj = cut(after(doc_proj, kv_half), x_bit, part_doc, 1)
    proj_near = [proj] + [flipped(proj, "tp", m) for m in masks[1:]]
    query_here = after(enc_query, proj)
    b_part, c_part = cut(query_here, x_bit, part_q, 0), cut(query_here, 2 + z_bit, part_q, 0)
    b_y = [flipped(b_part, "tp", m) for m in masks[1:]]
    c_y = [flipped(c_part, "tp", m) for m in masks[1:]]

    query_turned = after(enc_query, (b_part, c_part, kv_y[0])).T
    weights = []
    for w in kv_y:
        weights += [w, flipped(w, "rep", 1)]

    rows = slots * own_tokens
    lanes = 2 * kv_width * len(masks)
    out = [
        jax.ShapeDtypeStruct((rows, head_dim), F32),
        jax.ShapeDtypeStruct((slots, width), F32),
    ]
    scale, sums = pl.pallas_call(
        token_kernel,
        in_specs=[pl.BlockSpec(memory_space=pl.ANY)] + [pl.BlockSpec(memory_space=pltpu.VMEM)] * 3,
        out_shape=out,
        compiler_params=room(tokens, enc_gain, kv_rows, *out),
    )(query_turned, tokens, enc_gain, kv_rows)
    operands = (tokens, tokens_far, enc_gain, kv_rows, scale, sums, query_turned, *weights)
    out = [
        jax.ShapeDtypeStruct((2 * rows, lanes), BF16),
        jax.ShapeDtypeStruct((2 * rows, head_dim), BF16),
        jax.ShapeDtypeStruct(tokens.shape, BF16),
        jax.ShapeDtypeStruct(tokens.shape, BF16),
        jax.ShapeDtypeStruct((2 * rows, head_dim), F32),
        jax.ShapeDtypeStruct((slots, width), F32),
    ]
    kv, own, near, far, scale, mean = pl.pallas_call(
        functools.partial(keyvalue_kernel, length),
        out_shape=out,
        compiler_params=room(*operands, *out),
    )(*operands)
    kv_near = [kv] + [flipped(kv, "tp", m) for m in masks[1:]]

    proj_near = [after(p, weights[-1]) for p in proj_near]
    proj_all = proj_near + [flipped(p, "tp", 1) for p in proj_near]
    origin = masks + [m + 1 for m in masks]
    output_blocks = jnp.stack([cut(after(enc_output, weights[-1]), tp_index ^ m, block, 1) for m in range(n_tp)], axis=0)
    mean = mean.reshape(slots, n_tp, block)
    means = [lax.dynamic_index_in_dim(mean, tp_index ^ m, 1, keepdims=False) for m in masks]
    height = head_dim + -(-block // part_doc) * 2 * slots
    out = [jax.ShapeDtypeStruct((head_dim, part_doc), BF16)]
    out += [jax.ShapeDtypeStruct((height, part_doc), BF16) for _ in masks[1:]]
    w2, *packed = pl.pallas_call(
        functools.partial(product_kernel, origin),
        in_specs=[pl.BlockSpec(memory_space=pl.ANY)]
        + [pl.BlockSpec(memory_space=pltpu.VMEM)] * (n_tp + len(masks)),
        out_shape=out,
        compiler_params=room(output_blocks, *proj_all, *means, *out),
    )(kv, output_blocks, *proj_all, *means[1:])
    w2_all = [w2, flipped(w2, "rep", 1)]
    for m, p in zip(masks[1:], packed):
        w2_all += [flipped(p, "tp", m), flipped(w2_all[1], "tp", m)]

    count = 2 * lanes
    column = jnp.arange(count, dtype=jnp.int32)
    core = column // lanes
    mask_of = column % lanes // (2 * kv_width) * 2
    inner = column % (2 * kv_width)
    part_kv = kv_width // 2
    quarter = inner // part_kv
    swapped = quarter // 2 * 2 + (quarter % 2 ^ x_bit)
    inner = jnp.where(mask_of == 0, inner, swapped * part_kv + inner % part_kv)
    places = []
    for m in masks:
        target = (
            (mask_of ^ m) // group * (2 * head_dim)
            + inner // kv_width * head_dim
            + (tp_index ^ m ^ mask_of ^ core) % group * kv_width
            + inner % kv_width
        )
        places.append((target[:, None] == column[None, :]).astype(BF16))
    place = jnp.stack(places, axis=0)

    parts, b_rest, c_rest = [], [], []
    for q_b, q_c in zip(b_y, c_y):
        q_b, q_c = after((q_b, q_c), kv)
        parts += [q_b, q_c]
        b_rest.append(flipped(q_b, "rep", 1))
        c_rest.append(flipped(q_c, "rep", 2))
    operands = (near, far, *parts)
    out = [jax.ShapeDtypeStruct((2 * rows, head_dim), F32) for _ in masks[1:]]
    early = pl.pallas_call(
        query_kernel,
        in_specs=[pl.BlockSpec(memory_space=pl.ANY)]
        + [pl.BlockSpec(memory_space=pltpu.VMEM)] * len(operands),
        out_shape=out,
        compiler_params=room(*operands, *out),
    )(w2_all[1], *operands)

    kv_far = [flipped(after(k, (kv_near[1:], early, w2_all[-1])), "tp", 1) for k in kv_near]
    n = len(masks)
    groups = n_tp // group
    operands = (
        near,
        far,
        scale,
        own,
        *early,
        *b_rest,
        *c_rest,
        *kv_near,
        *kv_far,
        *w2_all,
        means[0],
        place,
        doc_proj,
    )
    scratch = [
        pltpu.VMEM((n, 2 * rows, head_dim), BF16),
        pltpu.VMEM((n, 2 * rows, 2 * lanes), BF16),
        pltpu.VMEM((slots, groups, n // groups * 2 * own_tokens, length), F32),
        pltpu.VMEM((slots, groups, n // groups, length), F32),
        pltpu.VMEM((n, slots, head_dim), F32),
        pltpu.VMEM((n, head_dim, doc_width), BF16),
    ]
    part = pl.pallas_call(
        functools.partial(attention_kernel, masks, group, length),
        out_shape=jax.ShapeDtypeStruct((slots, doc_width), F32),
        scratch_shapes=scratch,
        compiler_params=room(*operands, *scratch),
    )(*operands)

    part = part + flipped(part, "tp", 1) + flipped(part, "tp", 2) + flipped(part, "tp", 3)
    bit = 4
    while bit < n_tp:
        part = part + flipped(part, "tp", bit)
        bit *= 2
    bit = n_rep // 2
    while bit > 1:
        part = jnp.concatenate([part, flipped(part, "rep", bit)], axis=0)
        bit //= 2
    part_far = flipped(part, "rep", 1)

    seg_replica, doc_of_segment, doc_owner = after((seg_replica, doc_of_segment, doc_owner), kv)
    replica_of, rank = slot_table(seg_replica)
    row_of = owner_rows(doc_of_segment, doc_owner)
    owned = OWN_DOCS * DOC_MOST
    wanted = rep_index * owned + jnp.arange(owned, dtype=jnp.int32)
    matches = (row_of[None, :] == wanted[:, None]).astype(F32)
    apart, place_of, bit = replica_of ^ rep_index, 0, 1
    while bit < n_rep:
        place_of = place_of + (apart // bit % 2) * (n_rep // 2 // bit)
        bit *= 2
    at_slot = place_of * CAP + rank
    holds = (at_slot[:, None] == jnp.arange(n_rep * CAP, dtype=jnp.int32)[None, :]).astype(F32)
    select = jnp.dot(matches, holds)
    filled = jnp.sum(matches, axis=1)
    row = jnp.arange(owned, dtype=jnp.int32)
    same_doc = row[:, None] // DOC_MOST == row[None, :] // DOC_MOST
    allowed = same_doc & ((filled[None, :] > 0.5) | (row[:, None] == row[None, :]))

    operands = (
        part,
        part_far,
        select,
        allowed.astype(F32),
        filled[:, None],
        doc_gain[None, :],
        jnp.transpose(doc_qkv, (1, 2, 0)),
    )
    return pl.pallas_call(
        document_kernel,
        out_shape=jax.ShapeDtypeStruct((OWN_DOCS, DOC_MOST, doc_qkv.shape[2]), BF16),
        compiler_params=room(*operands),
    )(*operands)


def solution(mesh):
    in_specs = (
        P("rep", "tp", None),
        P(),
        P(),
        P(),
        P(),
        P(None, "tp"),
        P(None, None, "tp"),
        P("tp", None),
        P("tp", None),
        P(),
        P(None, None, "tp"),
    )
    out_specs = P("rep", None, "tp")
    return jax.shard_map(local, mesh=mesh, in_specs=in_specs, out_specs=out_specs, check_vma=False)
```
